256 devices in a mesh: batch: 128 (over y_hi, x, z, core), mp: 2 (over y_lo).
Axes of the slice: x: 4, y: 4 (y_hi: 2, y_lo: 2; y = y_hi * 2 + y_lo), z: 8, core: 2. Of those that a mesh axis runs over, the one named last changes fastest.
Arguments:
- image_feats: bfloat16 [16384, 1152], P('batch', 'mp'), may hold values from -4 to 4, as said below
- text_feats: bfloat16 [16384, 1152], P('batch', 'mp'), may hold values from -4 to 4, as said below
- image_proj: bfloat16 [1152, 768], P('mp'), may hold values from -0.1875 to 0.1875
- text_proj: bfloat16 [1152, 768], P('mp'), may hold values from -0.1875 to 0.1875
- image_bias: float32 [768], replicated, may hold values from -0.1 to 0.1
- text_bias: float32 [768], replicated, may hold values from -0.1 to 0.1
- image_ids: int32 [16384], replicated, may hold values from 0 to 8191
- text_ids: int32 [16384], replicated, may hold values from 0 to 8191
- log_scale: float32 [1], replicated, may hold values from 1.6 to 2.7
- logit_bias: float32 [1], replicated, may hold values from -4 to -1
Outputs:
- grad_image_feats: bfloat16 [16384, 1152], P('batch', 'mp')
- grad_text_feats: bfloat16 [16384, 1152], P('batch', 'mp')
- grad_image_proj: float32 [1152, 768], P('mp')
- grad_text_proj: float32 [1152, 768], P('mp')
- grad_image_bias: float32 [768], replicated
- grad_text_bias: float32 [768], replicated
The draws below stay inside these ranges and needn't reach their ends.
Inputs may be any that keep to these rules, and one draw needn't show every extreme that they name: `image_feats`: feature entries of each row. `text_feats`: feature entries of each row.
All inputs are finite; a program needn't handle non-finite values.
Results may differ from the reference program's by a relative error of at most 0.007.
Values may be sent and summed in bfloat16 or wider, within the bound.
No kernel may reach another device: no remote copies, remote signals or barrier semaphores. Data moves between devices by JAX's collectives and lax.ppermute only.
A program may use at most 128 MiB of HBM per device.

```python
import jax
import jax.numpy as jnp
from jax import lax

W = 1152
E = 768
B_DEV = 128
B = 16384
N_BATCH = 128


def draw_image_feats(key, part):
    key = jax.random.fold_in(key, 11)
    second = jax.random.fold_in(key, 1)
    values = jnp.clip(jax.random.normal(second, (B, W), jnp.float32), -4.0, 4.0)
    return values.astype(jnp.bfloat16)


def draw_text_feats(key, part):
    key = jax.random.fold_in(key, 23)
    second = jax.random.fold_in(key, 1)
    values = jnp.clip(jax.random.normal(second, (B, W), jnp.float32), -4.0, 4.0)
    return values.astype(jnp.bfloat16)


def place_ends(array, stream_key, low, top_value):
    index_at = [jax.random.randint(jax.random.fold_in(stream_key, axis), (), 0, length) for axis, length in enumerate(array.shape)]
    main_axis = array.shape.index(max(array.shape))
    neighbour = index_at[:main_axis] + [(index_at[main_axis] + 1) % array.shape[main_axis]] + index_at[main_axis + 1:]
    return array.at[tuple(index_at)].set(low).at[tuple(neighbour)].set(top_value)


def shard_levels(stream_key, shape, pieces, low, top_value):
    level = 1.0
    for axis_at, shards_of in pieces:
        heights = jax.random.uniform(jax.random.fold_in(jax.random.fold_in(stream_key, 6), axis_at), (shards_of,), jnp.float32, low / len(pieces), top_value / len(pieces))
        level = level * jnp.repeat(jnp.exp(heights), shape[axis_at] // shards_of).reshape((-1,) + (1,) * (len(shape) - 1 - axis_at))
    return level


def normal_values(rng, shape, scale, most, pieces=(), kind=jnp.bfloat16):
    array = jax.random.normal(rng, shape, jnp.float32) * scale
    if len(pieces) > 0:
        array = shard_levels(rng, shape, pieces, -0.22, 0.18) * array
    return jnp.clip(array, min=-most, max=most).astype(kind)


def setup_inputs(seed: int = 0) -> dict:
    keys = jax.random.split(jax.random.key(seed), 11)
    return {
        "image_feats": draw_image_feats(jax.random.fold_in(keys[10], 71), 0),
        "text_feats": draw_text_feats(jax.random.fold_in(keys[10], 71), 0),
        "image_proj": normal_values(keys[2], (W, E), W ** -0.5, 0.1875, ((0, 2),)),
        "text_proj": normal_values(keys[3], (W, E), W ** -0.5, 0.1875, ((0, 2),)),
        "image_bias": normal_values(keys[4], (E,), 0.02, 0.1, (), jnp.float32),
        "text_bias": normal_values(keys[5], (E,), 0.02, 0.1, (), jnp.float32),
        "image_ids": place_ends(jax.random.randint(keys[6], (B,), 0, B // 2), jax.random.fold_in(keys[6], 1), 0, (B // 2) - 1).astype(jnp.int32),
        "text_ids": place_ends(jax.random.randint(keys[7], (B,), 0, B // 2), jax.random.fold_in(keys[7], 1), 0, (B // 2) - 1).astype(jnp.int32),
        "log_scale": jnp.clip(jax.random.uniform(keys[8], (1,), jnp.float32, 1.6, 2.7), 1.6, 2.7),
        "logit_bias": jnp.clip(jax.random.uniform(keys[9], (1,), jnp.float32, -4.0, -1.0), -4.0, -1.0),
    }


def normalize_rows(raw_rows):
    row_norm = jnp.sqrt(lax.optimization_barrier(jnp.sum(raw_rows * raw_rows, axis=-1, keepdims=True)) + 1e-06)
    return (raw_rows / row_norm, row_norm)

def pair_coefs(left_emb, right_emb, left_ids, right_ids, logit_scale, shift_term):
    logits = logit_scale * jnp.dot(left_emb, right_emb.T, preferred_element_type=jnp.float32) + shift_term
    signs = jnp.where(left_ids[:, None] == right_ids[None, :], 1.0, -1.0).astype(logits.dtype)
    return (-logit_scale * signs * jax.nn.sigmoid(-signs * logits)).astype(jnp.bfloat16)

def raw_gradient(unit_grad, unit_rows, row_norm):
    return (unit_grad - unit_rows * lax.optimization_barrier(jnp.sum(unit_rows * unit_grad, axis=-1, keepdims=True))) / row_norm

def reference(image_feats, text_feats, image_proj, text_proj, image_bias, text_bias, image_ids, text_ids, log_scale, logit_bias):
    image_raw = jnp.dot(image_feats, image_proj, preferred_element_type=jnp.float32) + image_bias
    text_raw = jnp.dot(text_feats, text_proj, preferred_element_type=jnp.float32) + text_bias
    image_unit, image_norm = normalize_rows(image_raw)
    text_unit, text_norm = normalize_rows(text_raw)
    image_emb = image_unit.astype(jnp.bfloat16)
    text_emb = text_unit.astype(jnp.bfloat16)
    logit_scale = jnp.exp(log_scale[0])
    shift_term = logit_bias[0]

    def block_step(text_total, block_index):
        offset = (block_index * B_DEV).astype(jnp.int32)
        block_emb = lax.dynamic_slice_in_dim(image_emb, offset, B_DEV, 0)
        block_ids = lax.dynamic_slice_in_dim(image_ids, offset, B_DEV, 0)
        coefs = pair_coefs(block_emb, text_emb, block_ids, text_ids, logit_scale, shift_term)
        text_total = text_total + jnp.dot(coefs.T, block_emb, preferred_element_type=jnp.float32)
        return (text_total, jnp.dot(coefs, text_emb, preferred_element_type=jnp.float32))
    text_unit_grad, image_blocks = lax.scan(block_step, jnp.zeros((B, E), jnp.float32), jnp.arange(N_BATCH, dtype=jnp.int32))
    image_unit_grad = image_blocks.reshape(B, E)
    image_raw_grad = raw_gradient(image_unit_grad, image_unit, image_norm)
    text_raw_grad = raw_gradient(text_unit_grad, text_unit, text_norm)
    image_low = image_raw_grad.astype(jnp.bfloat16)
    text_low = text_raw_grad.astype(jnp.bfloat16)
    grad_image_feats = jnp.dot(image_low, image_proj.T, preferred_element_type=jnp.float32).astype(jnp.bfloat16)
    grad_text_feats = jnp.dot(text_low, text_proj.T, preferred_element_type=jnp.float32).astype(jnp.bfloat16)
    grad_image_proj = jnp.dot(image_feats.T, image_low, preferred_element_type=jnp.float32)
    grad_text_proj = jnp.dot(text_feats.T, text_low, preferred_element_type=jnp.float32)
    grad_image_bias = lax.optimization_barrier(jnp.sum(image_raw_grad, axis=0))
    grad_text_bias = lax.optimization_barrier(jnp.sum(text_raw_grad, axis=0))
    return (grad_image_feats, grad_text_feats, grad_image_proj, grad_text_proj, grad_image_bias, grad_text_bias)
```

```python
import functools

import jax
import jax.numpy as jnp
from jax import lax
from jax.experimental import pallas as pl
from jax.experimental.pallas import tpu as pltpu
from jax.sharding import Mesh
from jax.sharding import PartitionSpec as P

PLANE = ("yh", "x", "yl")
LOG2E = 1.4426950408889634
bf16 = jnp.bfloat16
f32 = jnp.float32


def exchange(value, axis):
    return lax.ppermute(value, axis, [(0, 1), (1, 0)])


def spread(block, axes, count):
    return lax.all_to_all(jnp.broadcast_to(block[None], (count,) + block.shape), axes, 0, 0)


def ordered(own, other, index):
    first = jnp.where(index == 0, own, other)
    second = jnp.where(index == 0, other, own)
    return jnp.concatenate([first, second], axis=0)


def pair_kernel(scal_ref, iid_ref, tid_ref, img_ref, txt_ref, gi_ref, gt_ref, acc_ref):
    step = pl.program_id(0)
    s2 = scal_ref[0]
    b2 = scal_ref[1]
    s = scal_ref[2]
    img = img_ref[...]
    txt = txt_ref[...]
    dots = lax.dot_general(img, txt, (((1,), (1,)), ((), ())), preferred_element_type=f32)
    turn = jnp.where(iid_ref[...] == tid_ref[...], 1.0, -1.0)
    coef = ((-s) * turn / (1.0 + jnp.exp2(turn * (dots * s2 + b2)))).astype(bf16)
    gi_ref[...] = jnp.dot(coef, txt, preferred_element_type=f32).astype(bf16)
    part = lax.dot_general(coef, img, (((0,), (0,)), ((), ())), preferred_element_type=f32)

    @pl.when(step == 0)
    def _():
        acc_ref[...] = part

    @pl.when(step > 0)
    def _():
        acc_ref[...] += part

    @pl.when(step == pl.num_programs(0) - 1)
    def _():
        gt_ref[...] = acc_ref[...].astype(bf16)


def pair_grads(scal, image_ids, text_ids, images, texts):
    rows, width = images.shape
    cols = texts.shape[0]
    block = min(256, rows)
    return pl.pallas_call(
        pair_kernel,
        grid=(rows // block,),
        in_specs=[
            pl.BlockSpec(memory_space=pltpu.SMEM),
            pl.BlockSpec((block, 1), lambda i: (i, 0)),
            pl.BlockSpec((1, cols), lambda i: (0, 0)),
            pl.BlockSpec((block, width), lambda i: (i, 0)),
            pl.BlockSpec((cols, width), lambda i: (0, 0)),
        ],
        out_specs=[
            pl.BlockSpec((block, width), lambda i: (i, 0)),
            pl.BlockSpec((cols, width), lambda i: (0, 0)),
        ],
        out_shape=[
            jax.ShapeDtypeStruct((rows, width), bf16),
            jax.ShapeDtypeStruct((cols, width), bf16),
        ],
        scratch_shapes=[pltpu.VMEM((cols, width), f32)],
        compiler_params=pltpu.CompilerParams(
            dimension_semantics=("arbitrary",), vmem_limit_bytes=40 * 1024 * 1024
        ),
        cost_estimate=pl.CostEstimate(
            flops=6 * rows * cols * width, bytes_accessed=8 * rows * width, transcendentals=2 * rows * cols
        ),
        name="pair_grads",
    )(scal, image_ids, text_ids, images, texts)


def raw_gradient(unit_grad, unit, norm):
    return (unit_grad - unit * jnp.sum(unit * unit_grad, axis=-1, keepdims=True)) / norm


def local(
    image_feats,
    text_feats,
    image_proj,
    text_proj,
    image_bias,
    text_bias,
    image_ids,
    text_ids,
    log_scale,
    logit_bias,
):
    rows, width = image_feats.shape
    emb = image_proj.shape[1]
    half = rows // 2
    yh, x, z, c, yl = (lax.axis_index(a) for a in ("yh", "x", "z", "c", "yl"))
    n_yh, n_x, n_z = (lax.axis_size(a) for a in ("yh", "x", "z"))
    n_plane = n_yh * n_x * 2

    other_feats = exchange(jnp.where(c == 0, text_feats, image_feats), "c")

    parts = jnp.stack(
        [
            jnp.dot(image_feats, image_proj, preferred_element_type=f32),
            jnp.dot(text_feats, text_proj, preferred_element_type=f32),
        ]
    ).reshape(2, 2, half, emb)
    kept = lax.dynamic_index_in_dim(parts, yl, 1, keepdims=False)
    sent = lax.dynamic_index_in_dim(parts, 1 - yl, 1, keepdims=False).astype(bf16)
    raw = kept + exchange(sent, "yl").astype(f32)
    raw = raw + jnp.stack([image_bias, text_bias])[:, None, :]
    norm = jnp.sqrt(jnp.sum(raw * raw, axis=-1, keepdims=True) + 1e-06)
    unit = raw / norm
    low = unit.astype(bf16)

    own_texts = lax.all_gather(low[1], "z", axis=0, tiled=True)
    images = spread(low[0], PLANE, n_plane).reshape(n_plane * half, emb)
    texts = jnp.concatenate([own_texts, exchange(own_texts, "c")], axis=0)

    grid = (n_yh, n_x, n_z, 2, 2, half)
    iids = image_ids.reshape(grid)
    iids = lax.dynamic_index_in_dim(iids, z, 2, keepdims=False)
    iids = lax.dynamic_index_in_dim(iids, c, 2, keepdims=False).reshape(-1, 1)
    tids = text_ids.reshape(grid)
    tids = lax.dynamic_index_in_dim(tids, yh, 0, keepdims=False)
    tids = lax.dynamic_index_in_dim(tids, x, 0, keepdims=False)
    tids = lax.dynamic_index_in_dim(tids, yl, 2, keepdims=False)
    tids = jnp.concatenate(
        [
            lax.dynamic_index_in_dim(tids, c, 1, keepdims=False).reshape(1, -1),
            lax.dynamic_index_in_dim(tids, 1 - c, 1, keepdims=False).reshape(1, -1),
        ],
        axis=1,
    )

    scale = jnp.exp(log_scale[0])
    scal = jnp.stack([scale * LOG2E, logit_bias[0] * LOG2E, scale])
    grad_images, grad_texts = pair_grads(scal, iids, tids, images, texts)

    n_own = n_z * half
    text_sum = grad_texts[:n_own].astype(f32) + exchange(grad_texts[n_own:], "c").astype(f32)
    text_pieces = lax.all_to_all(text_sum.astype(bf16).reshape(n_z, half, emb), "z", 0, 0)
    image_pieces = lax.all_to_all(grad_images.reshape(n_plane, half, emb), PLANE, 0, 0)
    unit_grad = jnp.stack(
        [
            jnp.sum(image_pieces.astype(f32), axis=0),
            jnp.sum(text_pieces.astype(f32), axis=0),
        ]
    )
    raw_grad = raw_gradient(unit_grad, unit, norm)
    bias_part = jnp.sum(raw_grad, axis=1)
    pack = jnp.concatenate(
        [raw_grad.reshape(2 * half, emb), bias_part, jnp.zeros((14, emb), f32)], axis=0
    ).astype(bf16)
    got = exchange(pack, "yl")
    image_low = ordered(pack[:half], got[:half], yl)
    text_low = ordered(pack[half : 2 * half], got[half : 2 * half], yl)
    bias_rows = pack[2 * half : 2 * half + 2].astype(f32) + got[2 * half : 2 * half + 2].astype(f32)

    grad_image_feats = lax.dot_general(
        image_low, image_proj, (((1,), (1,)), ((), ())), preferred_element_type=f32
    ).astype(bf16)
    grad_text_feats = lax.dot_general(
        text_low, text_proj, (((1,), (1,)), ((), ())), preferred_element_type=f32
    ).astype(bf16)

    extra = jnp.concatenate([bias_rows, jnp.zeros((14, emb), f32)], axis=0).astype(bf16)
    send = jnp.concatenate([jnp.where(c == 0, text_low, image_low), extra], axis=0)
    back = exchange(send, "c")
    own_feats = jnp.where(c == 0, image_feats, text_feats)
    own_low = jnp.where(c == 0, image_low, text_low)
    feats = jnp.concatenate([own_feats, other_feats], axis=0)
    lows = jnp.concatenate([own_low, back[:rows]], axis=0)
    weight = lax.dot_general(feats, lows, (((0,), (0,)), ((), ())), preferred_element_type=f32)
    bias_chip = bias_rows + back[rows : rows + 2].astype(f32)
    own_bias = lax.dynamic_slice_in_dim(bias_chip, c, 1, 0)
    n_square = n_yh * n_x
    tail = 8 * n_square
    payload = jnp.concatenate([weight, own_bias, jnp.zeros((tail - 1, emb), f32)], axis=0)
    deep = (width + tail) // n_square
    pieces = lax.all_to_all(payload.astype(bf16).reshape(n_square, deep, emb), ("yh", "x"), 0, 0)
    total = jnp.sum(pieces.astype(f32), axis=0)
    pieces = lax.all_to_all(total.astype(bf16).reshape(n_z, deep // n_z, emb), "z", 0, 0)
    total = jnp.sum(pieces.astype(f32), axis=0).astype(bf16)
    total = spread(total, "z", n_z).reshape(deep, emb)
    total = spread(total, ("yh", "x"), n_square).reshape(width + tail, emb)
    other = exchange(total[: width + 16], "c")
    image_total = jnp.where(c == 0, total[: width + 16], other).astype(f32)
    text_total = jnp.where(c == 0, other, total[: width + 16]).astype(f32)
    return (
        grad_image_feats,
        grad_text_feats,
        image_total[:width],
        text_total[:width],
        image_total[width],
        text_total[width],
    )


def solution(mesh):
    fine = Mesh(mesh.devices.reshape(2, 4, 8, 2, 2), ("yh", "x", "z", "c", "yl"))
    batch = ("yh", "x", "z", "c")
    in_specs = (
        P(batch, "yl"),
        P(batch, "yl"),
        P("yl", None),
        P("yl", None),
        P(),
        P(),
        P(),
        P(),
        P(),
        P(),
    )
    out_specs = (P(batch, "yl"), P(batch, "yl"), P("yl", None), P("yl", None), P(), P())
    return jax.shard_map(local, mesh=fine, in_specs=in_specs, out_specs=out_specs, check_vma=False)
```

```python
import functools

import jax
import jax.numpy as jnp
from jax import lax
from jax.experimental import pallas as pl
from jax.experimental.pallas import tpu as pltpu
from jax.sharding import Mesh
from jax.sharding import PartitionSpec as P

PLANE = ("yh", "x", "yl")
Z = ("zz", "z0")
BLOCK = ("yh", "x", "z0")
LOG2E = 1.4426950408889634
bf16 = jnp.bfloat16
f32 = jnp.float32


def exchange(value, axis):
    return lax.ppermute(value, axis, [(0, 1), (1, 0)])


def shift(value, axes, step, count):
    return lax.ppermute(value, axes, [(i, (i + step) % count) for i in range(count)])


PLACES = (0, 4, 6, 2, 7, 3, 1, 5)


def gather_ring(own, half):
    across = shift(own, Z, 4, 8)
    behind = shift(own, Z, 2, 8)
    ahead = shift(own, Z, 6, 8)
    two = jnp.concatenate([own, across], axis=0)
    return jnp.concatenate([two, behind, ahead, shift(two, Z, 1, 8), shift(two, Z, 7, 8)], axis=0)


def sum_ring(held, half):
    ahead = shift(held[6 * half :], Z, 1, 8).astype(f32)
    behind = shift(held[4 * half : 6 * half], Z, 7, 8).astype(f32)
    far = shift(held[2 * half : 3 * half], Z, 6, 8).astype(f32)
    near = shift(held[3 * half : 4 * half], Z, 2, 8).astype(f32)
    across = held[half : 2 * half].astype(f32) + ahead[half:] + behind[half:]
    across = shift(across.astype(bf16), Z, 4, 8).astype(f32)
    return held[:half].astype(f32) + ahead[:half] + behind[:half] + far + near + across


def spread(block, axes, count):
    return lax.all_to_all(jnp.broadcast_to(block[None], (count,) + block.shape), axes, 0, 0)


def ordered(own, other, index):
    first = jnp.where(index == 0, own, other)
    second = jnp.where(index == 0, other, own)
    return jnp.concatenate([first, second], axis=0)


def pair_kernel(scal_ref, iid_ref, tid_ref, img_ref, near_ref, far_ref, gi_ref, gn_ref, gf_ref, an_ref, af_ref):
    step = pl.program_id(0)
    s2 = scal_ref[0]
    b2 = scal_ref[1]
    s = scal_ref[2]
    img = img_ref[...]
    iid = iid_ref[...]
    total = None
    for side, (txt_ref, acc_ref) in enumerate(((near_ref, an_ref), (far_ref, af_ref))):
        txt = txt_ref[...]
        dots = lax.dot_general(img, txt, (((1,), (1,)), ((), ())), preferred_element_type=f32)
        turn = jnp.where(iid == tid_ref[side : side + 1, :], 1.0, -1.0)
        coef = ((-s) * turn / (1.0 + jnp.exp2(turn * (dots * s2 + b2)))).astype(bf16)
        grad = jnp.dot(coef, txt, preferred_element_type=f32)
        total = grad if total is None else total + grad
        part = lax.dot_general(coef, img, (((0,), (0,)), ((), ())), preferred_element_type=f32)

        @pl.when(step == 0)
        def _():
            acc_ref[...] = part

        @pl.when(step > 0)
        def _():
            acc_ref[...] += part

    gi_ref[...] = total.astype(bf16)

    @pl.when(step == pl.num_programs(0) - 1)
    def _():
        gn_ref[...] = an_ref[...].astype(bf16)
        gf_ref[...] = af_ref[...].astype(bf16)


def pair_grads(scal, image_ids, text_ids, images, near, far):
    rows, width = images.shape
    cols = near.shape[0]
    block = min(256, rows)
    whole = pl.BlockSpec((cols, width), lambda i: (0, 0))
    stripe = pl.BlockSpec((block, width), lambda i: (i, 0))
    return pl.pallas_call(
        pair_kernel,
        grid=(rows // block,),
        in_specs=[
            pl.BlockSpec(memory_space=pltpu.SMEM),
            pl.BlockSpec((block, 1), lambda i: (i, 0)),
            pl.BlockSpec((2, cols), lambda i: (0, 0)),
            stripe,
            whole,
            whole,
        ],
        out_specs=[stripe, whole, whole],
        out_shape=[
            jax.ShapeDtypeStruct((rows, width), bf16),
            jax.ShapeDtypeStruct((cols, width), bf16),
            jax.ShapeDtypeStruct((cols, width), bf16),
        ],
        scratch_shapes=[pltpu.VMEM((cols, width), f32), pltpu.VMEM((cols, width), f32)],
        compiler_params=pltpu.CompilerParams(
            dimension_semantics=("arbitrary",), vmem_limit_bytes=40 * 1024 * 1024
        ),
        cost_estimate=pl.CostEstimate(
            flops=12 * rows * cols * width, bytes_accessed=8 * rows * width, transcendentals=4 * rows * cols
        ),
        name="pair_grads",
    )(scal, image_ids, text_ids, images, near, far)


def raw_gradient(unit_grad, unit, norm):
    return (unit_grad - unit * jnp.sum(unit * unit_grad, axis=-1, keepdims=True)) / norm


def local(
    image_feats,
    text_feats,
    image_proj,
    text_proj,
    image_bias,
    text_bias,
    image_ids,
    text_ids,
    log_scale,
    logit_bias,
):
    rows, width = image_feats.shape
    emb = image_proj.shape[1]
    half = rows // 2
    yh, x, c, yl = (lax.axis_index(a) for a in ("yh", "x", "c", "yl"))
    z = lax.axis_index(Z)
    n_yh, n_x, n_z = 2, 4, 8
    n_plane = n_yh * n_x * 2
    n_block = n_yh * n_x * 2

    other_feats = exchange(jnp.where(c == 0, text_feats, image_feats), "c")

    grid = (n_yh, n_x, n_z, 2, 2, half)
    iids = image_ids.reshape(grid)
    iids = lax.dynamic_index_in_dim(iids, z, 2, keepdims=False)
    iids = lax.dynamic_index_in_dim(iids, c, 2, keepdims=False).reshape(-1, 1)
    tids = text_ids.reshape(grid)
    tids = lax.dynamic_index_in_dim(tids, yh, 0, keepdims=False)
    tids = lax.dynamic_index_in_dim(tids, x, 0, keepdims=False)
    tids = lax.dynamic_index_in_dim(tids, yl, 2, keepdims=False)
    tids = jnp.concatenate([tids, tids], axis=0)
    tids = lax.dynamic_slice_in_dim(tids, z, n_z, 0)
    tids = jnp.stack([tids[p] for p in PLACES])
    tids = jnp.stack(
        [
            lax.dynamic_index_in_dim(tids, c, 1, keepdims=False).reshape(-1),
            lax.dynamic_index_in_dim(tids, 1 - c, 1, keepdims=False).reshape(-1),
        ]
    )
    scale = jnp.exp(log_scale[0])
    scal = jnp.stack([scale * LOG2E, logit_bias[0] * LOG2E, scale])

    parts = jnp.stack(
        [
            jnp.dot(image_feats, image_proj, preferred_element_type=f32),
            jnp.dot(text_feats, text_proj, preferred_element_type=f32),
        ]
    ).reshape(2, 2, half, emb)
    kept = lax.dynamic_index_in_dim(parts, yl, 1, keepdims=False)
    sent = lax.dynamic_index_in_dim(parts, 1 - yl, 1, keepdims=False).astype(bf16)
    got = exchange(sent, "yl")
    got, iids, tids, scal, other_feats = lax.optimization_barrier((got, iids, tids, scal, other_feats))
    raw = kept + got.astype(f32)
    raw = raw + jnp.stack([image_bias, text_bias])[:, None, :]
    norm = jnp.sqrt(jnp.sum(raw * raw, axis=-1, keepdims=True) + 1e-06)
    unit = raw / norm
    low = unit.astype(bf16)

    near = gather_ring(low[1], half)
    images = spread(low[0], PLANE, n_plane).reshape(n_plane * half, emb)
    far = exchange(near, "c")
    grad_images, grad_near, grad_far = pair_grads(scal, iids, tids, images, near, far)

    image_pieces = lax.all_to_all(grad_images.reshape(n_plane, half, emb), PLANE, 0, 0)
    text_held = (grad_near.astype(f32) + exchange(grad_far, "c").astype(f32)).astype(bf16)
    text_sum = sum_ring(text_held, half)
    unit_grad = jnp.stack(
        [
            jnp.sum(image_pieces.astype(f32), axis=0),
            text_sum,
        ]
    )
    raw_grad = raw_gradient(unit_grad, unit, norm)
    bias_part = jnp.sum(raw_grad, axis=1)
    pack = jnp.concatenate(
        [raw_grad.reshape(2 * half, emb), bias_part, jnp.zeros((14, emb), f32)], axis=0
    ).astype(bf16)
    got = exchange(pack, "yl")
    image_low = ordered(pack[:half], got[:half], yl)
    text_low = ordered(pack[half : 2 * half], got[half : 2 * half], yl)
    bias_rows = pack[2 * half : 2 * half + 2].astype(f32) + got[2 * half : 2 * half + 2].astype(f32)

    grad_image_feats = lax.dot_general(
        image_low, image_proj, (((1,), (1,)), ((), ())), preferred_element_type=f32
    ).astype(bf16)
    grad_text_feats = lax.dot_general(
        text_low, text_proj, (((1,), (1,)), ((), ())), preferred_element_type=f32
    ).astype(bf16)

    extra = jnp.concatenate([bias_rows, jnp.zeros((14, emb), f32)], axis=0).astype(bf16)
    send = jnp.concatenate([jnp.where(c == 0, text_low, image_low), extra], axis=0)
    back = exchange(send, "c")
    own_feats = jnp.where(c == 0, image_feats, text_feats)
    own_low = jnp.where(c == 0, image_low, text_low)
    feats = jnp.concatenate([own_feats, other_feats], axis=0)
    lows = jnp.concatenate([own_low, back[:rows]], axis=0)
    weight = lax.dot_general(feats, lows, (((0,), (0,)), ((), ())), preferred_element_type=f32)
    bias_chip = bias_rows + back[rows : rows + 2].astype(f32)
    own_bias = lax.dynamic_slice_in_dim(bias_chip, c, 1, 0)
    tail = 4 * n_block
    payload = jnp.concatenate([weight, own_bias, jnp.zeros((tail - 1, emb), f32)], axis=0)
    deep = (width + tail) // n_block
    pieces = lax.all_to_all(payload.astype(bf16).reshape(n_block, deep, emb), BLOCK, 0, 0)
    pieces, grad_image_feats, grad_text_feats = lax.optimization_barrier(
        (pieces, grad_image_feats, grad_text_feats)
    )
    part = jnp.sum(pieces.astype(f32), axis=0).astype(bf16)
    one, two, three = (shift(part, "zz", d, 4).astype(f32) for d in (1, 2, 3))
    total = ((part.astype(f32) + two) + (one + three)).astype(bf16)
    total = spread(total, BLOCK, n_block).reshape(width + tail, emb)
    other = exchange(total, "c")
    return (
        grad_image_feats,
        grad_text_feats,
        jnp.where(c == 0, total[:width], other[:width]).astype(f32),
        jnp.where(c == 0, other[:width], total[:width]).astype(f32),
        jnp.where(c == 0, total[width], other[width]).astype(f32),
        jnp.where(c == 0, other[width], total[width]).astype(f32),
    )


def solution(mesh):
    fine = Mesh(mesh.devices.reshape(2, 4, 4, 2, 2, 2), ("yh", "x", "zz", "z0", "c", "yl"))
    batch = ("yh", "x", "zz", "z0", "c")
    in_specs = (
        P(batch, "yl"),
        P(batch, "yl"),
        P("yl", None),
        P("yl", None),
        P(),
        P(),
        P(),
        P(),
        P(),
        P(),
    )
    out_specs = (P(batch, "yl"), P(batch, "yl"), P("yl", None), P("yl", None), P(), P())
    return jax.shard_map(local, mesh=fine, in_specs=in_specs, out_specs=out_specs, check_vma=False)
```

```python
import functools

import jax
import jax.numpy as jnp
from jax import lax
from jax.experimental import pallas as pl
from jax.experimental.pallas import tpu as pltpu
from jax.sharding import Mesh
from jax.sharding import PartitionSpec as P

PLANE = ("yh", "x", "yl")
Z = ("zz", "z0")
BLOCK = ("yh", "x", "z0")
LOG2E = 1.4426950408889634
bf16 = jnp.bfloat16
f32 = jnp.float32


def exchange(value, axis):
    return lax.ppermute(value, axis, [(0, 1), (1, 0)])


def shift(value, axes, step, count):
    return lax.ppermute(value, axes, [(i, (i + step) % count) for i in range(count)])


PLACES = (0, 4, 6, 2, 7, 3, 1, 5)


def gather_ring(own, half):
    across = shift(own, Z, 4, 8)
    behind = shift(own, Z, 2, 8)
    ahead = shift(own, Z, 6, 8)
    two = jnp.concatenate([own, across], axis=0)
    return jnp.concatenate([two, behind, ahead, shift(two, Z, 1, 8), shift(two, Z, 7, 8)], axis=0)


def sum_ring(held, half):
    ahead = shift(held[6 * half :], Z, 1, 8).astype(f32)
    behind = shift(held[4 * half : 6 * half], Z, 7, 8).astype(f32)
    far = shift(held[2 * half : 3 * half], Z, 6, 8).astype(f32)
    near = shift(held[3 * half : 4 * half], Z, 2, 8).astype(f32)
    across = held[half : 2 * half].astype(f32) + ahead[half:] + behind[half:]
    across = shift(across.astype(bf16), Z, 4, 8).astype(f32)
    return held[:half].astype(f32) + ahead[:half] + behind[:half] + far + near + across


def spread(block, axes, count):
    return lax.all_to_all(jnp.broadcast_to(block[None], (count,) + block.shape), axes, 0, 0)


def ordered(own, other, index):
    first = jnp.where(index == 0, own, other)
    second = jnp.where(index == 0, other, own)
    return jnp.concatenate([first, second], axis=0)


def pair_kernel(scal_ref, iid_ref, tid_ref, img_ref, near_ref, far_ref, gi_ref, cn_ref, cf_ref):
    rows = img_ref.shape[0]
    block = min(512, rows)
    s2 = scal_ref[0]
    b2 = scal_ref[1]
    s = scal_ref[2]
    for i in range(rows // block):
        part = pl.ds(i * block, block)
        img = img_ref[part, :]
        iid = jnp.broadcast_to(iid_ref[:, i * block : (i + 1) * block], (8, block)).T[:, :1]
        for side, (txt_ref, out_ref) in enumerate(((near_ref, cn_ref), (far_ref, cf_ref))):
            dots = lax.dot_general(img, txt_ref[...], (((1,), (1,)), ((), ())), preferred_element_type=f32)
            turn = jnp.where(iid == tid_ref[side : side + 1, :], 1.0, -1.0)
            coef = (-s) * turn / (1.0 + jnp.exp2(turn * (dots * s2 + b2)))
            out_ref[part, :] = coef.astype(bf16)
    gi_ref[...] = (
        jnp.dot(cn_ref[...], near_ref[...], preferred_element_type=f32)
        + jnp.dot(cf_ref[...], far_ref[...], preferred_element_type=f32)
    ).astype(bf16)


def pair_coefs(scal, image_ids, text_ids, images, near, far):
    rows, width = images.shape
    cols = near.shape[0]
    vmem = pl.BlockSpec(memory_space=pltpu.VMEM)
    return pl.pallas_call(
        pair_kernel,
        in_specs=[pl.BlockSpec(memory_space=pltpu.SMEM)] + [vmem] * 5,
        out_specs=[vmem] * 3,
        out_shape=[
            jax.ShapeDtypeStruct((rows, width), bf16),
            jax.ShapeDtypeStruct((rows, cols), bf16),
            jax.ShapeDtypeStruct((rows, cols), bf16),
        ],
        compiler_params=pltpu.CompilerParams(vmem_limit_bytes=40 * 1024 * 1024),
        cost_estimate=pl.CostEstimate(
            flops=8 * rows * cols * width, bytes_accessed=12 * rows * width, transcendentals=4 * rows * cols
        ),
        name="pair_coefs",
    )(scal, image_ids, text_ids, images, near, far)


def text_kernel(coef_ref, img_ref, out_ref):
    out_ref[...] = lax.dot_general(
        coef_ref[...], img_ref[...], (((0,), (0,)), ((), ())), preferred_element_type=f32
    ).astype(bf16)


def text_grads(coef, images):
    rows, width = images.shape
    cols = coef.shape[1]
    vmem = pl.BlockSpec(memory_space=pltpu.VMEM)
    return pl.pallas_call(
        text_kernel,
        in_specs=[vmem] * 2,
        out_specs=vmem,
        out_shape=jax.ShapeDtypeStruct((cols, width), bf16),
        compiler_params=pltpu.CompilerParams(vmem_limit_bytes=20 * 1024 * 1024),
        cost_estimate=pl.CostEstimate(
            flops=2 * rows * cols * width, bytes_accessed=4 * rows * width, transcendentals=0
        ),
        name="text_grads",
    )(coef, images)


def pick(parts, index):
    return lax.dynamic_index_in_dim(parts, index, 0, keepdims=False)


def normalized(raw):
    norm = jnp.sqrt(jnp.sum(raw * raw, axis=-1, keepdims=True) + 1e-06)
    return raw / norm, norm


def raw_gradient(unit_grad, unit, norm):
    return (unit_grad - unit * jnp.sum(unit * unit_grad, axis=-1, keepdims=True)) / norm


def local(
    image_feats,
    text_feats,
    image_proj,
    text_proj,
    image_bias,
    text_bias,
    image_ids,
    text_ids,
    log_scale,
    logit_bias,
):
    rows, width = image_feats.shape
    emb = image_proj.shape[1]
    half = rows // 2
    yh, x, c, yl = (lax.axis_index(a) for a in ("yh", "x", "c", "yl"))
    z = lax.axis_index(Z)
    n_yh, n_x, n_z = 2, 4, 8
    n_plane = n_yh * n_x * 2
    n_block = n_yh * n_x * 2

    other_feats = exchange(jnp.where(c == 0, text_feats, image_feats), "c")

    grid = (n_yh, n_x, n_z, 2, 2, half)
    iids = image_ids.reshape(grid)
    iids = lax.dynamic_index_in_dim(iids, z, 2, keepdims=False)
    iids = lax.dynamic_index_in_dim(iids, c, 2, keepdims=False).reshape(1, -1)
    tids = text_ids.reshape(grid)
    tids = lax.dynamic_index_in_dim(tids, yh, 0, keepdims=False)
    tids = lax.dynamic_index_in_dim(tids, x, 0, keepdims=False)
    tids = lax.dynamic_index_in_dim(tids, yl, 2, keepdims=False)
    tids = jnp.concatenate([tids, tids], axis=0)
    tids = lax.dynamic_slice_in_dim(tids, z, n_z, 0)
    tids = jnp.stack([tids[p] for p in PLACES])
    tids = jnp.stack(
        [
            lax.dynamic_index_in_dim(tids, c, 1, keepdims=False).reshape(-1),
            lax.dynamic_index_in_dim(tids, 1 - c, 1, keepdims=False).reshape(-1),
        ]
    )
    scale = jnp.exp(log_scale[0])
    scal = jnp.stack([scale * LOG2E, logit_bias[0] * LOG2E, scale])

    image_part = jnp.dot(image_feats, image_proj, preferred_element_type=f32).reshape(2, half, emb)
    text_part = jnp.dot(text_feats, text_proj, preferred_element_type=f32).reshape(2, half, emb)
    image_got = exchange(pick(image_part, 1 - yl).astype(bf16), "yl")
    text_got = exchange(pick(text_part, 1 - yl).astype(bf16), "yl")
    image_got, iids, tids, scal, other_feats = lax.optimization_barrier(
        (image_got, iids, tids, scal, other_feats)
    )
    image_unit, image_norm = normalized(pick(image_part, yl) + image_got.astype(f32) + image_bias)
    image_copies = jnp.broadcast_to(image_unit.astype(bf16)[None], (n_plane, half, emb))
    image_copies, text_got = lax.optimization_barrier((image_copies, text_got))
    text_unit, text_norm = normalized(pick(text_part, yl) + text_got.astype(f32) + text_bias)

    images = lax.all_to_all(image_copies, PLANE, 0, 0).reshape(n_plane * half, emb)
    near = gather_ring(text_unit.astype(bf16), half)
    far = exchange(near, "c")
    grad_images, coef_near, coef_far = pair_coefs(scal, iids, tids, images, near, far)

    image_pieces = lax.all_to_all(grad_images.reshape(n_plane, half, emb), PLANE, 0, 0)
    grad_far = exchange(text_grads(coef_far, images), "c")
    grad_near = text_grads(coef_near, images)
    text_held = (grad_near.astype(f32) + grad_far.astype(f32)).astype(bf16)
    text_sum = sum_ring(text_held, half)
    image_sum = jnp.sum(image_pieces.astype(f32), axis=0)
    image_grad = raw_gradient(image_sum, image_unit, image_norm)
    text_grad = raw_gradient(text_sum, text_unit, text_norm)
    pack = jnp.concatenate(
        [
            image_grad,
            text_grad,
            jnp.sum(image_grad, axis=0, keepdims=True),
            jnp.sum(text_grad, axis=0, keepdims=True),
            jnp.zeros((14, emb), f32),
        ],
        axis=0,
    ).astype(bf16)
    got = exchange(pack, "yl")
    image_low = ordered(pack[:half], got[:half], yl)
    text_low = ordered(pack[half : 2 * half], got[half : 2 * half], yl)
    bias_rows = pack[2 * half : 2 * half + 2].astype(f32) + got[2 * half : 2 * half + 2].astype(f32)

    grad_image_feats = lax.dot_general(
        image_low, image_proj, (((1,), (1,)), ((), ())), preferred_element_type=f32
    ).astype(bf16)
    grad_text_feats = lax.dot_general(
        text_low, text_proj, (((1,), (1,)), ((), ())), preferred_element_type=f32
    ).astype(bf16)

    extra = jnp.concatenate([bias_rows, jnp.zeros((14, emb), f32)], axis=0).astype(bf16)
    send = jnp.concatenate([jnp.where(c == 0, text_low, image_low), extra], axis=0)
    back = exchange(send, "c")
    own_feats = jnp.where(c == 0, image_feats, text_feats)
    own_low = jnp.where(c == 0, image_low, text_low)
    feats = jnp.concatenate([own_feats, other_feats], axis=0)
    lows = jnp.concatenate([own_low, back[:rows]], axis=0)
    weight = lax.dot_general(feats, lows, (((0,), (0,)), ((), ())), preferred_element_type=f32)
    bias_chip = bias_rows + back[rows : rows + 2].astype(f32)
    own_bias = lax.dynamic_slice_in_dim(bias_chip, c, 1, 0)
    tail = 4 * n_block
    payload = jnp.concatenate([weight, own_bias, jnp.zeros((tail - 1, emb), f32)], axis=0)
    deep = (width + tail) // n_block
    pieces = lax.all_to_all(payload.astype(bf16).reshape(n_block, deep, emb), BLOCK, 0, 0)
    pieces, grad_image_feats, grad_text_feats = lax.optimization_barrier(
        (pieces, grad_image_feats, grad_text_feats)
    )
    part = jnp.sum(pieces.astype(f32), axis=0).astype(bf16)
    one, two, three = (shift(part, "zz", d, 4).astype(f32) for d in (1, 2, 3))
    total = ((part.astype(f32) + two) + (one + three)).astype(bf16)
    total = spread(total, BLOCK, n_block).reshape(width + tail, emb)
    other = exchange(total, "c")
    return (
        grad_image_feats,
        grad_text_feats,
        jnp.where(c == 0, total[:width], other[:width]).astype(f32),
        jnp.where(c == 0, other[:width], total[:width]).astype(f32),
        jnp.where(c == 0, total[width], other[width]).astype(f32),
        jnp.where(c == 0, other[width], total[width]).astype(f32),
    )


def solution(mesh):
    fine = Mesh(mesh.devices.reshape(2, 4, 4, 2, 2, 2), ("yh", "x", "zz", "z0", "c", "yl"))
    batch = ("yh", "x", "zz", "z0", "c")
    in_specs = (
        P(batch, "yl"),
        P(batch, "yl"),
        P("yl", None),
        P("yl", None),
        P(),
        P(),
        P(),
        P(),
        P(),
        P(),
    )
    out_specs = (P(batch, "yl"), P(batch, "yl"), P("yl", None), P("yl", None), P(), P())
    return jax.shard_map(local, mesh=fine, in_specs=in_specs, out_specs=out_specs, check_vma=False)
```

```python
import functools

import jax
import jax.numpy as jnp
from jax import lax
from jax.experimental import pallas as pl
from jax.experimental.pallas import tpu as pltpu
from jax.sharding import Mesh
from jax.sharding import PartitionSpec as P

PLANE = ("yh", "x", "yl")
Z = ("zz", "z0")
BLOCK = ("yh", "x", "z0")
LIMIT = 24 * 1024 * 1024
LOG2E = 1.4426950408889634
bf16 = jnp.bfloat16
f32 = jnp.float32


def exchange(value, axis):
    return lax.ppermute(value, axis, [(0, 1), (1, 0)])


def shift(value, axes, step, count):
    return lax.ppermute(value, axes, [(i, (i + step) % count) for i in range(count)])


PLACES = (0, 4, 6, 2, 7, 3, 1, 5)


def gather_ring(own, half):
    across = shift(own, Z, 4, 8)
    behind = shift(own, Z, 2, 8)
    ahead = shift(own, Z, 6, 8)
    two = jnp.concatenate([own, across], axis=0)
    return jnp.concatenate([two, behind, ahead, shift(two, Z, 1, 8), shift(two, Z, 7, 8)], axis=0)


def sum_ring(held, half):
    ahead = shift(held[6 * half :], Z, 1, 8).astype(f32)
    behind = shift(held[4 * half : 6 * half], Z, 7, 8).astype(f32)
    far = shift(held[2 * half : 3 * half], Z, 6, 8).astype(f32)
    near = shift(held[3 * half : 4 * half], Z, 2, 8).astype(f32)
    across = held[half : 2 * half].astype(f32) + ahead[half:] + behind[half:]
    across = shift(across.astype(bf16), Z, 4, 8).astype(f32)
    return held[:half].astype(f32) + ahead[:half] + behind[:half] + far + near + across


def spread(block, axes, count):
    return lax.all_to_all(jnp.broadcast_to(block[None], (count,) + block.shape), axes, 0, 0)


def ordered(own, other, index):
    first = jnp.where(index == 0, own, other)
    second = jnp.where(index == 0, other, own)
    return jnp.concatenate([first, second], axis=0)


def coefs_of(scal_ref, iid_ref, tid_ref, img_ref, txt_ref, out_ref):
    rows = img_ref.shape[0]
    block = min(512, rows)
    s2 = scal_ref[0]
    b2 = scal_ref[1]
    s = scal_ref[2]
    for i in range(rows // block):
        part = pl.ds(i * block, block)
        iid = jnp.broadcast_to(iid_ref[:, i * block : (i + 1) * block], (8, block)).T[:, :1]
        dots = lax.dot_general(
            img_ref[part, :], txt_ref[...], (((1,), (1,)), ((), ())), preferred_element_type=f32
        )
        turn = jnp.where(iid == tid_ref[...], 1.0, -1.0)
        coef = (-s) * turn / (1.0 + jnp.exp2(turn * (dots * s2 + b2)))
        out_ref[part, :] = coef.astype(bf16)


def near_kernel(scal_ref, iid_ref, tid_ref, img_ref, near_ref, cn_ref):
    coefs_of(scal_ref, iid_ref, tid_ref, img_ref, near_ref, cn_ref)


def far_kernel(scal_ref, iid_ref, tid_ref, img_ref, far_ref, near_ref, cn_ref, gi_ref, cf_ref):
    coefs_of(scal_ref, iid_ref, tid_ref, img_ref, far_ref, cf_ref)
    gi_ref[...] = (
        jnp.dot(cn_ref[...], near_ref[...], preferred_element_type=f32)
        + jnp.dot(cf_ref[...], far_ref[...], preferred_element_type=f32)
    ).astype(bf16)


VMEM = pl.BlockSpec(memory_space=pltpu.VMEM)
SMEM = pl.BlockSpec(memory_space=pltpu.SMEM)


def near_coefs(scal, image_ids, text_ids, images, near):
    rows, width = images.shape
    cols = near.shape[0]
    return pl.pallas_call(
        near_kernel,
        in_specs=[SMEM] + [VMEM] * 4,
        out_specs=VMEM,
        out_shape=jax.ShapeDtypeStruct((rows, cols), bf16),
        compiler_params=pltpu.CompilerParams(vmem_limit_bytes=LIMIT),
        cost_estimate=pl.CostEstimate(
            flops=2 * rows * cols * width, bytes_accessed=4 * rows * width, transcendentals=2 * rows * cols
        ),
        name="near_coefs",
    )(scal, image_ids, text_ids, images, near)


def far_coefs(scal, image_ids, text_ids, images, far, near, coef_near):
    rows, width = images.shape
    cols = near.shape[0]
    return pl.pallas_call(
        far_kernel,
        in_specs=[SMEM] + [VMEM] * 6,
        out_specs=[VMEM] * 2,
        out_shape=[
            jax.ShapeDtypeStruct((rows, width), bf16),
            jax.ShapeDtypeStruct((rows, cols), bf16),
        ],
        compiler_params=pltpu.CompilerParams(vmem_limit_bytes=LIMIT),
        cost_estimate=pl.CostEstimate(
            flops=6 * rows * cols * width, bytes_accessed=8 * rows * width, transcendentals=2 * rows * cols
        ),
        name="far_coefs",
    )(scal, image_ids, text_ids, images, far, near, coef_near)


def text_kernel(coef_ref, img_ref, out_ref):
    out_ref[...] = lax.dot_general(
        coef_ref[...], img_ref[...], (((0,), (0,)), ((), ())), preferred_element_type=f32
    ).astype(bf16)


def text_grads(coef, images):
    rows, width = images.shape
    cols = coef.shape[1]
    return pl.pallas_call(
        text_kernel,
        in_specs=[VMEM] * 2,
        out_specs=VMEM,
        out_shape=jax.ShapeDtypeStruct((cols, width), bf16),
        compiler_params=pltpu.CompilerParams(vmem_limit_bytes=LIMIT),
        cost_estimate=pl.CostEstimate(flops=0, bytes_accessed=0, transcendentals=0),
        name="text_grads",
    )(coef, images)


def pick(parts, index):
    return lax.dynamic_index_in_dim(parts, index, 0, keepdims=False)


def normalized(raw):
    norm = jnp.sqrt(jnp.sum(raw * raw, axis=-1, keepdims=True) + 1e-06)
    return raw / norm, norm


def raw_gradient(unit_grad, unit, norm):
    return (unit_grad - unit * jnp.sum(unit * unit_grad, axis=-1, keepdims=True)) / norm


def local(
    image_feats,
    text_feats,
    image_proj,
    text_proj,
    image_bias,
    text_bias,
    image_ids,
    text_ids,
    log_scale,
    logit_bias,
):
    rows, width = image_feats.shape
    emb = image_proj.shape[1]
    half = rows // 2
    yh, x, c, yl = (lax.axis_index(a) for a in ("yh", "x", "c", "yl"))
    z = lax.axis_index(Z)
    n_yh, n_x, n_z = 2, 4, 8
    n_plane = n_yh * n_x * 2
    n_block = n_yh * n_x * 2

    grid = (n_yh, n_x, n_z, 2, 2, half)
    iids = image_ids.reshape(grid)
    iids = lax.dynamic_index_in_dim(iids, z, 2, keepdims=False)
    iids = lax.dynamic_index_in_dim(iids, c, 2, keepdims=False).reshape(1, -1)
    tids = text_ids.reshape(grid)
    tids = lax.dynamic_index_in_dim(tids, yh, 0, keepdims=False)
    tids = lax.dynamic_index_in_dim(tids, x, 0, keepdims=False)
    tids = lax.dynamic_index_in_dim(tids, yl, 2, keepdims=False)
    tids = jnp.concatenate([tids, tids], axis=0)
    tids = lax.dynamic_slice_in_dim(tids, z, n_z, 0)
    tids = jnp.stack([tids[p] for p in PLACES])
    near_ids = lax.dynamic_index_in_dim(tids, c, 1, keepdims=False).reshape(1, -1)
    far_ids = lax.dynamic_index_in_dim(tids, 1 - c, 1, keepdims=False).reshape(1, -1)
    scale = jnp.exp(log_scale[0])
    scal = jnp.stack([scale * LOG2E, logit_bias[0] * LOG2E, scale])

    image_part = jnp.dot(image_feats, image_proj, preferred_element_type=f32).reshape(2, half, emb)
    text_part = jnp.dot(text_feats, text_proj, preferred_element_type=f32).reshape(2, half, emb)
    image_got = exchange(pick(image_part, 1 - yl).astype(bf16), "yl")
    image_got, iids, near_ids, far_ids, scal = lax.optimization_barrier(
        (image_got, iids, near_ids, far_ids, scal)
    )
    image_unit, image_norm = normalized(pick(image_part, yl) + image_got.astype(f32) + image_bias)
    image_copies = jnp.broadcast_to(image_unit.astype(bf16)[None], (n_plane, half, emb))
    image_copies, text_send, image_late, text_late = lax.optimization_barrier(
        (image_copies, pick(text_part, 1 - yl).astype(bf16), image_feats, text_feats)
    )
    text_got = exchange(text_send, "yl")
    text_unit, text_norm = normalized(pick(text_part, yl) + text_got.astype(f32) + text_bias)

    images = lax.all_to_all(image_copies, PLANE, 0, 0).reshape(n_plane * half, emb)
    near = gather_ring(text_unit.astype(bf16), half)
    own_feats = jnp.where(c == 0, image_late, text_late)
    other_feats = exchange(jnp.where(c == 0, text_late, image_late), "c")
    images, near, own_feats, other_feats = lax.optimization_barrier((images, near, own_feats, other_feats))
    far = exchange(near, "c")
    coef_near = near_coefs(scal, iids, near_ids, images, near)
    grad_images, coef_far = far_coefs(scal, iids, far_ids, images, far, near, coef_near)

    image_pieces = lax.all_to_all(grad_images.reshape(n_plane, half, emb), PLANE, 0, 0)
    grad_far = exchange(text_grads(coef_far, images), "c")
    grad_near = text_grads(coef_near, images)
    text_held = (grad_near.astype(f32) + grad_far.astype(f32)).astype(bf16)
    text_sum = sum_ring(text_held, half)
    image_sum = jnp.sum(image_pieces.astype(f32), axis=0)
    image_grad = raw_gradient(image_sum, image_unit, image_norm)
    text_grad = raw_gradient(text_sum, text_unit, text_norm)
    pack = jnp.concatenate(
        [
            image_grad,
            text_grad,
            jnp.sum(image_grad, axis=0, keepdims=True),
            jnp.sum(text_grad, axis=0, keepdims=True),
            jnp.zeros((14, emb), f32),
        ],
        axis=0,
    ).astype(bf16)
    got = exchange(pack, "yl")
    image_low = ordered(pack[:half], got[:half], yl)
    text_low = ordered(pack[half : 2 * half], got[half : 2 * half], yl)
    bias_rows = pack[2 * half : 2 * half + 2].astype(f32) + got[2 * half : 2 * half + 2].astype(f32)

    grad_image_feats = lax.dot_general(
        image_low, image_proj, (((1,), (1,)), ((), ())), preferred_element_type=f32
    ).astype(bf16)
    grad_text_feats = lax.dot_general(
        text_low, text_proj, (((1,), (1,)), ((), ())), preferred_element_type=f32
    ).astype(bf16)

    extra = jnp.concatenate([bias_rows, jnp.zeros((14, emb), f32)], axis=0).astype(bf16)
    send = jnp.concatenate([jnp.where(c == 0, text_low, image_low), extra], axis=0)
    back = exchange(send, "c")
    own_low = jnp.where(c == 0, image_low, text_low)
    feats = jnp.concatenate([own_feats, other_feats], axis=0)
    lows = jnp.concatenate([own_low, back[:rows]], axis=0)
    weight = lax.dot_general(feats, lows, (((0,), (0,)), ((), ())), preferred_element_type=f32)
    bias_chip = bias_rows + back[rows : rows + 2].astype(f32)
    own_bias = lax.dynamic_slice_in_dim(bias_chip, c, 1, 0)
    tail = 4 * n_block
    payload = jnp.concatenate([weight, own_bias, jnp.zeros((tail - 1, emb), f32)], axis=0)
    deep = (width + tail) // n_block
    pieces = lax.all_to_all(payload.astype(bf16).reshape(n_block, deep, emb), BLOCK, 0, 0)
    pieces, grad_image_feats, grad_text_feats = lax.optimization_barrier(
        (pieces, grad_image_feats, grad_text_feats)
    )
    part = jnp.sum(pieces.astype(f32), axis=0).astype(bf16)
    one, two, three = (shift(part, "zz", d, 4).astype(f32) for d in (1, 2, 3))
    total = ((part.astype(f32) + two) + (one + three)).astype(bf16)
    total = spread(total, BLOCK, n_block).reshape(width + tail, emb)
    other = exchange(total, "c")
    return (
        grad_image_feats,
        grad_text_feats,
        jnp.where(c == 0, total[:width], other[:width]).astype(f32),
        jnp.where(c == 0, other[:width], total[:width]).astype(f32),
        jnp.where(c == 0, total[width], other[width]).astype(f32),
        jnp.where(c == 0, other[width], total[width]).astype(f32),
    )


def solution(mesh):
    fine = Mesh(mesh.devices.reshape(2, 4, 4, 2, 2, 2), ("yh", "x", "zz", "z0", "c", "yl"))
    batch = ("yh", "x", "zz", "z0", "c")
    in_specs = (
        P(batch, "yl"),
        P(batch, "yl"),
        P("yl", None),
        P("yl", None),
        P(),
        P(),
        P(),
        P(),
        P(),
        P(),
    )
    out_specs = (P(batch, "yl"), P(batch, "yl"), P("yl", None), P("yl", None), P(), P())
    return jax.shard_map(local, mesh=fine, in_specs=in_specs, out_specs=out_specs, check_vma=False)
```

```python
import functools

import jax
import jax.numpy as jnp
from jax import lax
from jax.experimental import pallas as pl
from jax.experimental.pallas import tpu as pltpu
from jax.sharding import Mesh
from jax.sharding import PartitionSpec as P

PLANE = ("yh", "x", "yl")
Z = ("zz", "z0")
BLOCK = ("yh", "x", "z0")
LIMIT = 24 * 1024 * 1024
LOG2E = 1.4426950408889634
bf16 = jnp.bfloat16
f32 = jnp.float32


def exchange(value, axis):
    return lax.ppermute(value, axis, [(0, 1), (1, 0)])


def shift(value, axes, step, count):
    return lax.ppermute(value, axes, [(i, (i + step) % count) for i in range(count)])


PLACES = (0, 4, 6, 2, 7, 3, 1, 5)


def gather_ring(own, half):
    across = shift(own, Z, 4, 8)
    behind = shift(own, Z, 2, 8)
    ahead = shift(own, Z, 6, 8)
    two = jnp.concatenate([own, across], axis=0)
    return jnp.concatenate([two, behind, ahead, shift(two, Z, 1, 8), shift(two, Z, 7, 8)], axis=0)


def sum_ring(held, half):
    ahead = shift(held[6 * half :], Z, 1, 8).astype(f32)
    behind = shift(held[4 * half : 6 * half], Z, 7, 8).astype(f32)
    far = shift(held[2 * half : 3 * half], Z, 6, 8).astype(f32)
    near = shift(held[3 * half : 4 * half], Z, 2, 8).astype(f32)
    across = held[half : 2 * half].astype(f32) + ahead[half:] + behind[half:]
    across = shift(across.astype(bf16), Z, 4, 8).astype(f32)
    return held[:half].astype(f32) + ahead[:half] + behind[:half] + far + near + across


def spread(block, axes, count):
    return lax.all_to_all(jnp.broadcast_to(block[None], (count,) + block.shape), axes, 0, 0)


def ordered(own, other, index):
    first = jnp.where(index == 0, own, other)
    second = jnp.where(index == 0, other, own)
    return jnp.concatenate([first, second], axis=0)


def coefs_of(scal_ref, iid_ref, tid_ref, img_ref, txt_ref, out_ref):
    rows = img_ref.shape[0]
    block = min(512, rows)
    s2 = scal_ref[0]
    b2 = scal_ref[1]
    s = scal_ref[2]
    for i in range(rows // block):
        part = pl.ds(i * block, block)
        iid = jnp.broadcast_to(iid_ref[:, i * block : (i + 1) * block], (8, block)).T[:, :1]
        dots = lax.dot_general(
            img_ref[part, :], txt_ref[...], (((1,), (1,)), ((), ())), preferred_element_type=f32
        )
        turn = jnp.where(iid == tid_ref[...], 1.0, -1.0)
        coef = (-s) * turn / (1.0 + jnp.exp2(turn * (dots * s2 + b2)))
        out_ref[part, :] = coef.astype(bf16)


def pair_kernel(scal_ref, iid_ref, tid_ref, img_ref, txt_ref, coef_ref, grad_ref):
    coefs_of(scal_ref, iid_ref, tid_ref, img_ref, txt_ref, coef_ref)
    grad_ref[...] = lax.dot_general(
        coef_ref[...], img_ref[...], (((0,), (0,)), ((), ())), preferred_element_type=f32
    ).astype(bf16)


def image_kernel(cn_ref, cf_ref, near_ref, far_ref, gi_ref):
    gi_ref[...] = (
        jnp.dot(cn_ref[...], near_ref[...], preferred_element_type=f32)
        + jnp.dot(cf_ref[...], far_ref[...], preferred_element_type=f32)
    ).astype(bf16)


VMEM = pl.BlockSpec(memory_space=pltpu.VMEM)
SMEM = pl.BlockSpec(memory_space=pltpu.SMEM)


def pair_block(scal, image_ids, text_ids, images, texts, name):
    rows, width = images.shape
    cols = texts.shape[0]
    return pl.pallas_call(
        pair_kernel,
        in_specs=[SMEM] + [VMEM] * 4,
        out_specs=[VMEM] * 2,
        out_shape=[jax.ShapeDtypeStruct((rows, cols), bf16), jax.ShapeDtypeStruct((cols, width), bf16)],
        compiler_params=pltpu.CompilerParams(vmem_limit_bytes=LIMIT),
        cost_estimate=pl.CostEstimate(
            flops=4 * rows * cols * width, bytes_accessed=6 * rows * width, transcendentals=2 * rows * cols
        ),
        name=name,
    )(scal, image_ids, text_ids, images, texts)


def image_grads(coef_near, coef_far, near, far):
    rows, cols = coef_near.shape
    width = near.shape[1]
    return pl.pallas_call(
        image_kernel,
        in_specs=[VMEM] * 4,
        out_specs=VMEM,
        out_shape=jax.ShapeDtypeStruct((rows, width), bf16),
        compiler_params=pltpu.CompilerParams(vmem_limit_bytes=LIMIT),
        cost_estimate=pl.CostEstimate(
            flops=4 * rows * cols * width, bytes_accessed=6 * rows * width, transcendentals=0
        ),
        name="image_grads",
    )(coef_near, coef_far, near, far)


def weight_kernel(own_ref, other_ref, low_ref, back_ref, bias_ref, out_ref):
    width, rows = own_ref.shape
    out_ref[:width, :] = (
        jnp.dot(own_ref[...], low_ref[...], preferred_element_type=f32)
        + jnp.dot(other_ref[...], back_ref[:rows, :], preferred_element_type=f32)
    ).astype(bf16)
    depth = out_ref.shape[0] - width
    row = lax.broadcasted_iota(jnp.int32, (depth, out_ref.shape[1]), 0)
    out_ref[width:, :] = jnp.where(row == 0, bias_ref[...], 0.0).astype(bf16)


def weight_grads(own_feats, other_feats, low, back, bias, tail):
    width, rows = own_feats.shape
    emb = low.shape[1]
    return pl.pallas_call(
        weight_kernel,
        in_specs=[VMEM] * 5,
        out_specs=VMEM,
        out_shape=jax.ShapeDtypeStruct((width + tail, emb), bf16),
        compiler_params=pltpu.CompilerParams(vmem_limit_bytes=LIMIT),
        cost_estimate=pl.CostEstimate(
            flops=4 * rows * width * emb, bytes_accessed=4 * width * emb, transcendentals=0
        ),
        name="weight_grads",
    )(own_feats, other_feats, low, back, bias)


def pick(parts, index):
    return lax.dynamic_index_in_dim(parts, index, 0, keepdims=False)


def normalized(raw):
    norm = jnp.sqrt(jnp.sum(raw * raw, axis=-1, keepdims=True) + 1e-06)
    return raw / norm, norm


def raw_gradient(unit_grad, unit, norm):
    return (unit_grad - unit * jnp.sum(unit * unit_grad, axis=-1, keepdims=True)) / norm


def local(
    image_feats,
    text_feats,
    image_proj,
    text_proj,
    image_bias,
    text_bias,
    image_ids,
    text_ids,
    log_scale,
    logit_bias,
):
    rows, width = image_feats.shape
    emb = image_proj.shape[1]
    half = rows // 2
    yh, x, c, yl = (lax.axis_index(a) for a in ("yh", "x", "c", "yl"))
    z = lax.axis_index(Z)
    n_yh, n_x, n_z = 2, 4, 8
    n_plane = n_yh * n_x * 2
    n_block = n_yh * n_x * 2

    grid = (n_yh, n_x, n_z, 2, 2, half)
    iids = image_ids.reshape(grid)
    iids = lax.dynamic_index_in_dim(iids, z, 2, keepdims=False)
    iids = lax.dynamic_index_in_dim(iids, c, 2, keepdims=False).reshape(1, -1)
    tids = text_ids.reshape(grid)
    tids = lax.dynamic_index_in_dim(tids, yh, 0, keepdims=False)
    tids = lax.dynamic_index_in_dim(tids, x, 0, keepdims=False)
    tids = lax.dynamic_index_in_dim(tids, yl, 2, keepdims=False)
    tids = jnp.concatenate([tids, tids], axis=0)
    tids = lax.dynamic_slice_in_dim(tids, z, n_z, 0)
    tids = jnp.stack([tids[p] for p in PLACES])
    near_ids = lax.dynamic_index_in_dim(tids, c, 1, keepdims=False).reshape(1, -1)
    far_ids = lax.dynamic_index_in_dim(tids, 1 - c, 1, keepdims=False).reshape(1, -1)
    scale = jnp.exp(log_scale[0])
    scal = jnp.stack([scale * LOG2E, logit_bias[0] * LOG2E, scale])

    image_part = jnp.dot(image_feats, image_proj, preferred_element_type=f32).reshape(2, half, emb)
    text_part = jnp.dot(text_feats, text_proj, preferred_element_type=f32).reshape(2, half, emb)
    image_got = exchange(pick(image_part, 1 - yl).astype(bf16), "yl")
    image_got, iids, near_ids, far_ids, scal = lax.optimization_barrier(
        (image_got, iids, near_ids, far_ids, scal)
    )
    image_raw = pick(image_part, yl) + image_got.astype(f32) + image_bias
    image_unit, image_norm = normalized(image_raw)
    image_copies = jnp.broadcast_to(image_unit.astype(bf16)[None], (n_plane, half, emb))
    image_copies, text_send, image_late, text_late = lax.optimization_barrier(
        (image_copies, pick(text_part, 1 - yl).astype(bf16), image_feats.T, text_feats.T)
    )
    text_got = exchange(text_send, "yl")
    text_raw = pick(text_part, yl) + text_got.astype(f32) + text_bias
    text_unit, text_norm = normalized(text_raw)

    images = lax.all_to_all(image_copies, PLANE, 0, 0).reshape(n_plane * half, emb)
    near = gather_ring(text_unit.astype(bf16), half)
    own_feats = jnp.where(c == 0, image_late, text_late)
    other_feats = exchange(jnp.where(c == 0, text_late, image_late), "c")
    images, near, own_feats, other_feats = lax.optimization_barrier((images, near, own_feats, other_feats))
    far = exchange(near, "c")
    coef_near, grad_near = pair_block(scal, iids, near_ids, images, near, "near_pairs")
    far, coef_near, grad_near = lax.optimization_barrier((far, coef_near, grad_near))
    coef_far, grad_far = pair_block(scal, iids, far_ids, images, far, "far_pairs")
    grad_images = image_grads(coef_near, coef_far, near, far)

    grad_far = exchange(grad_far, "c")
    image_pieces = lax.all_to_all(grad_images.reshape(n_plane, half, emb), PLANE, 0, 0)
    text_held = (grad_near.astype(f32) + grad_far.astype(f32)).astype(bf16)
    text_sum = sum_ring(text_held, half)
    image_sum = jnp.sum(image_pieces.astype(f32), axis=0)
    image_grad = raw_gradient(image_sum, image_unit, image_norm)
    text_grad = raw_gradient(text_sum, text_unit, text_norm)
    pack = jnp.concatenate(
        [
            image_grad,
            text_grad,
            jnp.sum(image_grad, axis=0, keepdims=True),
            jnp.sum(text_grad, axis=0, keepdims=True),
            jnp.zeros((14, emb), f32),
        ],
        axis=0,
    ).astype(bf16)
    got = exchange(pack, "yl")
    image_low = ordered(pack[:half], got[:half], yl)
    text_low = ordered(pack[half : 2 * half], got[half : 2 * half], yl)
    bias_rows = pack[2 * half : 2 * half + 2].astype(f32) + got[2 * half : 2 * half + 2].astype(f32)

    grad_image_feats = lax.dot_general(
        image_low, image_proj, (((1,), (1,)), ((), ())), preferred_element_type=f32
    ).astype(bf16)
    grad_text_feats = lax.dot_general(
        text_low, text_proj, (((1,), (1,)), ((), ())), preferred_element_type=f32
    ).astype(bf16)

    extra = jnp.concatenate([bias_rows, jnp.zeros((14, emb), f32)], axis=0).astype(bf16)
    send = jnp.concatenate([jnp.where(c == 0, text_low, image_low), extra], axis=0)
    back = exchange(send, "c")
    own_low = jnp.where(c == 0, image_low, text_low)
    bias_chip = bias_rows + back[rows : rows + 2].astype(f32)
    own_bias = lax.dynamic_slice_in_dim(bias_chip, c, 1, 0)
    tail = 4 * n_block
    payload = weight_grads(own_feats, other_feats, own_low, back, own_bias, tail)
    deep = (width + tail) // n_block
    pieces = lax.all_to_all(payload.reshape(n_block, deep, emb), BLOCK, 0, 0)
    pieces, grad_image_feats, grad_text_feats = lax.optimization_barrier(
        (pieces, grad_image_feats, grad_text_feats)
    )
    part = jnp.sum(pieces.astype(f32), axis=0).astype(bf16)
    one, two, three = (shift(part, "zz", d, 4).astype(f32) for d in (1, 2, 3))
    total = ((part.astype(f32) + two) + (one + three)).astype(bf16)
    total = spread(total, BLOCK, n_block).reshape(width + tail, emb)
    other = exchange(total, "c")
    return (
        grad_image_feats,
        grad_text_feats,
        jnp.where(c == 0, total[:width], other[:width]).astype(f32),
        jnp.where(c == 0, other[:width], total[:width]).astype(f32),
        jnp.where(c == 0, total[width], other[width]).astype(f32),
        jnp.where(c == 0, other[width], total[width]).astype(f32),
    )


def solution(mesh):
    fine = Mesh(mesh.devices.reshape(2, 4, 4, 2, 2, 2), ("yh", "x", "zz", "z0", "c", "yl"))
    batch = ("yh", "x", "zz", "z0", "c")
    in_specs = (
        P(batch, "yl"),
        P(batch, "yl"),
        P("yl", None),
        P("yl", None),
        P(),
        P(),
        P(),
        P(),
        P(),
        P(),
    )
    out_specs = (P(batch, "yl"), P(batch, "yl"), P("yl", None), P("yl", None), P(), P())
    return jax.shard_map(local, mesh=fine, in_specs=in_specs, out_specs=out_specs, check_vma=False)
```

```python
import functools

import jax
import jax.numpy as jnp
from jax import lax
from jax.experimental import pallas as pl
from jax.experimental.pallas import tpu as pltpu
from jax.sharding import Mesh
from jax.sharding import PartitionSpec as P

PLANE = ("yh", "x", "yl")
Z = ("zz", "z0")
BLOCK = ("yh", "x", "z0")
LIMIT = 24 * 1024 * 1024
LOG2E = 1.4426950408889634
bf16 = jnp.bfloat16
f32 = jnp.float32


def exchange(value, axis):
    return lax.ppermute(value, axis, [(0, 1), (1, 0)])


def shift(value, axes, step, count):
    return lax.ppermute(value, axes, [(i, (i + step) % count) for i in range(count)])


PLACES = (0, 4, 6, 2, 7, 3, 1, 5)


def gather_ring(own, half):
    across = shift(own, Z, 4, 8)
    behind = shift(own, Z, 2, 8)
    ahead = shift(own, Z, 6, 8)
    two = jnp.concatenate([own, across], axis=0)
    return jnp.concatenate([two, behind, ahead, shift(two, Z, 1, 8), shift(two, Z, 7, 8)], axis=0)


def sum_ring(held, half):
    ahead = shift(held[6 * half :], Z, 1, 8)
    behind = shift(held[4 * half : 6 * half], Z, 7, 8)
    ahead, behind, two = lax.optimization_barrier((ahead, behind, held[2 * half : 4 * half]))
    ahead, behind = ahead.astype(f32), behind.astype(f32)
    far = shift(two[:half], Z, 6, 8).astype(f32)
    near = shift(two[half:], Z, 2, 8).astype(f32)
    across = held[half : 2 * half].astype(f32) + ahead[half:] + behind[half:]
    across = shift(across.astype(bf16), Z, 4, 8).astype(f32)
    return held[:half].astype(f32) + ahead[:half] + behind[:half] + far + near + across


def spread(block, axes, count):
    return lax.all_to_all(jnp.broadcast_to(block[None], (count,) + block.shape), axes, 0, 0)


def ordered(own, other, index):
    first = jnp.where(index == 0, own, other)
    second = jnp.where(index == 0, other, own)
    return jnp.concatenate([first, second], axis=0)


def coefs_of(scal_ref, iid_ref, tid_ref, img_ref, txt_ref, out_ref):
    rows = img_ref.shape[0]
    block = min(512, rows)
    s2 = scal_ref[0]
    b2 = scal_ref[1]
    s = scal_ref[2]
    for i in range(rows // block):
        part = pl.ds(i * block, block)
        iid = jnp.broadcast_to(iid_ref[:, i * block : (i + 1) * block], (8, block)).T[:, :1]
        dots = lax.dot_general(
            img_ref[part, :], txt_ref[...], (((1,), (1,)), ((), ())), preferred_element_type=f32
        )
        turn = jnp.where(iid == tid_ref[...], 1.0, -1.0)
        coef = (-s) * turn / (1.0 + jnp.exp2(turn * (dots * s2 + b2)))
        out_ref[part, :] = coef.astype(bf16)


def pair_kernel(scal_ref, iid_ref, tid_ref, img_ref, txt_ref, coef_ref, grad_ref):
    coefs_of(scal_ref, iid_ref, tid_ref, img_ref, txt_ref, coef_ref)
    grad_ref[...] = lax.dot_general(
        coef_ref[...], img_ref[...], (((0,), (0,)), ((), ())), preferred_element_type=f32
    ).astype(bf16)


def image_kernel(cn_ref, cf_ref, near_ref, far_ref, gi_ref):
    gi_ref[...] = (
        jnp.dot(cn_ref[...], near_ref[...], preferred_element_type=f32)
        + jnp.dot(cf_ref[...], far_ref[...], preferred_element_type=f32)
    ).astype(bf16)


VMEM = pl.BlockSpec(memory_space=pltpu.VMEM)
SMEM = pl.BlockSpec(memory_space=pltpu.SMEM)


def pair_block(scal, image_ids, text_ids, images, texts, name):
    rows, width = images.shape
    cols = texts.shape[0]
    return pl.pallas_call(
        pair_kernel,
        in_specs=[SMEM] + [VMEM] * 4,
        out_specs=[VMEM] * 2,
        out_shape=[jax.ShapeDtypeStruct((rows, cols), bf16), jax.ShapeDtypeStruct((cols, width), bf16)],
        compiler_params=pltpu.CompilerParams(vmem_limit_bytes=LIMIT),
        cost_estimate=pl.CostEstimate(
            flops=4 * rows * cols * width, bytes_accessed=6 * rows * width, transcendentals=2 * rows * cols
        ),
        name=name,
    )(scal, image_ids, text_ids, images, texts)


def image_grads(coef_near, coef_far, near, far):
    rows, cols = coef_near.shape
    width = near.shape[1]
    block = min(256, rows)
    whole = pl.BlockSpec((cols, width), lambda i: (0, 0))
    part = pl.BlockSpec((block, cols), lambda i: (i, 0))
    return pl.pallas_call(
        image_kernel,
        grid=(rows // block,),
        in_specs=[part, part, whole, whole],
        out_specs=pl.BlockSpec((block, width), lambda i: (i, 0)),
        out_shape=jax.ShapeDtypeStruct((rows, width), bf16),
        compiler_params=pltpu.CompilerParams(
            dimension_semantics=("arbitrary",), vmem_limit_bytes=LIMIT
        ),
        cost_estimate=pl.CostEstimate(
            flops=4 * rows * cols * width, bytes_accessed=6 * rows * width, transcendentals=0
        ),
        name="image_grads",
    )(coef_near, coef_far, near, far)


def weight_kernel(own_ref, other_ref, low_ref, back_ref, bias_ref, out_ref):
    width, rows = own_ref.shape
    out_ref[:width, :] = (
        jnp.dot(own_ref[...], low_ref[...], preferred_element_type=f32)
        + jnp.dot(other_ref[...], back_ref[:rows, :], preferred_element_type=f32)
    ).astype(bf16)
    depth = out_ref.shape[0] - width
    row = lax.broadcasted_iota(jnp.int32, (depth, out_ref.shape[1]), 0)
    out_ref[width:, :] = jnp.where(row == 0, bias_ref[...], 0.0).astype(bf16)


def weight_grads(own_feats, other_feats, low, back, bias, tail):
    width, rows = own_feats.shape
    emb = low.shape[1]
    return pl.pallas_call(
        weight_kernel,
        in_specs=[VMEM] * 5,
        out_specs=VMEM,
        out_shape=jax.ShapeDtypeStruct((width + tail, emb), bf16),
        compiler_params=pltpu.CompilerParams(vmem_limit_bytes=LIMIT),
        cost_estimate=pl.CostEstimate(
            flops=4 * rows * width * emb, bytes_accessed=4 * width * emb, transcendentals=0
        ),
        name="weight_grads",
    )(own_feats, other_feats, low, back, bias)


def pick(parts, index):
    return lax.dynamic_index_in_dim(parts, index, 0, keepdims=False)


def normalized(raw):
    norm = jnp.sqrt(jnp.sum(raw * raw, axis=-1, keepdims=True) + 1e-06)
    return raw / norm, norm


def raw_gradient(unit_grad, unit, norm):
    return (unit_grad - unit * jnp.sum(unit * unit_grad, axis=-1, keepdims=True)) / norm


def local(
    image_feats,
    text_feats,
    image_proj,
    text_proj,
    image_bias,
    text_bias,
    image_ids,
    text_ids,
    log_scale,
    logit_bias,
):
    rows, width = image_feats.shape
    emb = image_proj.shape[1]
    half = rows // 2
    yh, x, c, yl = (lax.axis_index(a) for a in ("yh", "x", "c", "yl"))
    z = lax.axis_index(Z)
    n_yh, n_x, n_z = 2, 4, 8
    n_plane = n_yh * n_x * 2
    n_block = n_yh * n_x * 2

    grid = (n_yh, n_x, n_z, 2, 2, half)
    iids = image_ids.reshape(grid)
    iids = lax.dynamic_index_in_dim(iids, z, 2, keepdims=False)
    iids = lax.dynamic_index_in_dim(iids, c, 2, keepdims=False).reshape(1, -1)
    tids = text_ids.reshape(grid)
    tids = lax.dynamic_index_in_dim(tids, yh, 0, keepdims=False)
    tids = lax.dynamic_index_in_dim(tids, x, 0, keepdims=False)
    tids = lax.dynamic_index_in_dim(tids, yl, 2, keepdims=False)
    tids = jnp.concatenate([tids, tids], axis=0)
    tids = lax.dynamic_slice_in_dim(tids, z, n_z, 0)
    tids = jnp.stack([tids[p] for p in PLACES])
    near_ids = lax.dynamic_index_in_dim(tids, c, 1, keepdims=False).reshape(1, -1)
    far_ids = lax.dynamic_index_in_dim(tids, 1 - c, 1, keepdims=False).reshape(1, -1)
    scale = jnp.exp(log_scale[0])
    scal = jnp.stack([scale * LOG2E, logit_bias[0] * LOG2E, scale])

    image_part = jnp.dot(image_feats, image_proj, preferred_element_type=f32).reshape(2, half, emb)
    text_part = jnp.dot(text_feats, text_proj, preferred_element_type=f32).reshape(2, half, emb)
    image_got = exchange(pick(image_part, 1 - yl).astype(bf16), "yl")
    image_got, iids, near_ids, far_ids, scal = lax.optimization_barrier(
        (image_got, iids, near_ids, far_ids, scal)
    )
    image_raw = pick(image_part, yl) + image_got.astype(f32) + image_bias
    image_unit, image_norm = normalized(image_raw)
    image_copies = jnp.broadcast_to(image_unit.astype(bf16)[None], (n_plane, half, emb))
    image_copies, text_send, image_late, text_late = lax.optimization_barrier(
        (image_copies, pick(text_part, 1 - yl).astype(bf16), image_feats.T, text_feats.T)
    )
    text_got = exchange(text_send, "yl")
    text_raw = pick(text_part, yl) + text_got.astype(f32) + text_bias
    text_unit, text_norm = normalized(text_raw)

    images = lax.all_to_all(image_copies, PLANE, 0, 0).reshape(n_plane * half, emb)
    near = gather_ring(text_unit.astype(bf16), half)
    own_feats = jnp.where(c == 0, image_late, text_late)
    other_feats = exchange(jnp.where(c == 0, text_late, image_late), "c")
    images, near, own_feats, other_feats = lax.optimization_barrier((images, near, own_feats, other_feats))
    far = exchange(near, "c")
    coef_near, grad_near = pair_block(scal, iids, near_ids, images, near, "near_pairs")
    far, coef_near, grad_near = lax.optimization_barrier((far, coef_near, grad_near))
    coef_far, grad_far = pair_block(scal, iids, far_ids, images, far, "far_pairs")
    grad_images = image_grads(coef_near, coef_far, near, far)

    grad_far = exchange(grad_far, "c")
    image_pieces = lax.all_to_all(grad_images.reshape(n_plane, half, emb), PLANE, 0, 0)
    text_held = (grad_near.astype(f32) + grad_far.astype(f32)).astype(bf16)
    text_sum = sum_ring(text_held, half)
    image_sum = jnp.sum(image_pieces.astype(f32), axis=0)
    image_grad = raw_gradient(image_sum, image_unit, image_norm)
    text_grad = raw_gradient(text_sum, text_unit, text_norm)
    pack = jnp.concatenate(
        [
            image_grad,
            text_grad,
            jnp.sum(image_grad, axis=0, keepdims=True),
            jnp.sum(text_grad, axis=0, keepdims=True),
            jnp.zeros((14, emb), f32),
        ],
        axis=0,
    ).astype(bf16)
    got = exchange(pack, "yl")
    image_low = ordered(pack[:half], got[:half], yl)
    text_low = ordered(pack[half : 2 * half], got[half : 2 * half], yl)
    bias_rows = pack[2 * half : 2 * half + 2].astype(f32) + got[2 * half : 2 * half + 2].astype(f32)

    grad_image_feats = lax.dot_general(
        image_low, image_proj, (((1,), (1,)), ((), ())), preferred_element_type=f32
    ).astype(bf16)
    grad_text_feats = lax.dot_general(
        text_low, text_proj, (((1,), (1,)), ((), ())), preferred_element_type=f32
    ).astype(bf16)

    extra = jnp.concatenate([bias_rows, jnp.zeros((14, emb), f32)], axis=0).astype(bf16)
    send = jnp.concatenate([jnp.where(c == 0, text_low, image_low), extra], axis=0)
    back = exchange(send, "c")
    own_low = jnp.where(c == 0, image_low, text_low)
    bias_chip = bias_rows + back[rows : rows + 2].astype(f32)
    own_bias = lax.dynamic_slice_in_dim(bias_chip, c, 1, 0)
    tail = 4 * n_block
    payload = weight_grads(own_feats, other_feats, own_low, back, own_bias, tail)
    deep = (width + tail) // n_block
    pieces = lax.all_to_all(payload.reshape(n_block, deep, emb), BLOCK, 0, 0)
    pieces, grad_image_feats, grad_text_feats = lax.optimization_barrier(
        (pieces, grad_image_feats, grad_text_feats)
    )
    part = jnp.sum(pieces.astype(f32), axis=0).astype(bf16)
    one, two, three = (shift(part, "zz", d, 4).astype(f32) for d in (1, 2, 3))
    total = ((part.astype(f32) + two) + (one + three)).astype(bf16)
    total = spread(total, BLOCK, n_block).reshape(width + tail, emb)
    other = exchange(total, "c")
    return (
        grad_image_feats,
        grad_text_feats,
        jnp.where(c == 0, total[:width], other[:width]).astype(f32),
        jnp.where(c == 0, other[:width], total[:width]).astype(f32),
        jnp.where(c == 0, total[width], other[width]).astype(f32),
        jnp.where(c == 0, other[width], total[width]).astype(f32),
    )


def solution(mesh):
    fine = Mesh(mesh.devices.reshape(2, 4, 4, 2, 2, 2), ("yh", "x", "zz", "z0", "c", "yl"))
    batch = ("yh", "x", "zz", "z0", "c")
    in_specs = (
        P(batch, "yl"),
        P(batch, "yl"),
        P("yl", None),
        P("yl", None),
        P(),
        P(),
        P(),
        P(),
        P(),
        P(),
    )
    out_specs = (P(batch, "yl"), P(batch, "yl"), P("yl", None), P("yl", None), P(), P())
    return jax.shard_map(local, mesh=fine, in_specs=in_specs, out_specs=out_specs, check_vma=False)
```

```python
import functools

import jax
import jax.numpy as jnp
from jax import lax
from jax.experimental import pallas as pl
from jax.experimental.pallas import tpu as pltpu
from jax.sharding import Mesh
from jax.sharding import PartitionSpec as P

PLANE = ("yh", "x", "yl")
Z = ("zz", "z0")
BLOCK = ("yh", "x", "z0")
LIMIT = 24 * 1024 * 1024
LOG2E = 1.4426950408889634
bf16 = jnp.bfloat16
f32 = jnp.float32


def exchange(value, axis):
    return lax.ppermute(value, axis, [(0, 1), (1, 0)])


def shift(value, axes, step, count):
    return lax.ppermute(value, axes, [(i, (i + step) % count) for i in range(count)])


PLACES = (0, 4, 6, 2, 7, 3, 1, 5)


def gather_ring(own, half):
    across = shift(own, Z, 4, 8)
    behind = shift(own, Z, 2, 8)
    ahead = shift(own, Z, 6, 8)
    two = jnp.concatenate([own, across], axis=0)
    return jnp.concatenate([two, behind, ahead, shift(two, Z, 1, 8), shift(two, Z, 7, 8)], axis=0)


def sum_ring(held, half):
    ahead = shift(held[6 * half :], Z, 1, 8).astype(f32)
    behind = shift(held[4 * half : 6 * half], Z, 7, 8).astype(f32)
    far = shift(held[2 * half : 3 * half], Z, 6, 8).astype(f32)
    near = shift(held[3 * half : 4 * half], Z, 2, 8).astype(f32)
    across = held[half : 2 * half].astype(f32) + ahead[half:] + behind[half:]
    across = shift(across.astype(bf16), Z, 4, 8).astype(f32)
    return held[:half].astype(f32) + ahead[:half] + behind[:half] + far + near + across


def spread(block, axes, count):
    return lax.all_to_all(jnp.broadcast_to(block[None], (count,) + block.shape), axes, 0, 0)


def ordered(own, other, index):
    first = jnp.where(index == 0, own, other)
    second = jnp.where(index == 0, other, own)
    return jnp.concatenate([first, second], axis=0)


def coefs_of(scal_ref, iid_ref, tid_ref, img_ref, txt_ref, out_ref):
    rows = img_ref.shape[0]
    block = min(512, rows)
    s2 = scal_ref[0]
    b2 = scal_ref[1]
    s = scal_ref[2]
    for i in range(rows // block):
        part = pl.ds(i * block, block)
        iid = jnp.broadcast_to(iid_ref[:, i * block : (i + 1) * block], (8, block)).T[:, :1]
        dots = lax.dot_general(
            img_ref[part, :], txt_ref[...], (((1,), (1,)), ((), ())), preferred_element_type=f32
        )
        turn = jnp.where(iid == tid_ref[...], 1.0, -1.0)
        coef = (-s) * turn / (1.0 + jnp.exp2(turn * (dots * s2 + b2)))
        out_ref[part, :] = coef.astype(bf16)


def pair_kernel(scal_ref, iid_ref, tid_ref, img_ref, txt_ref, coef_ref, grad_ref):
    coefs_of(scal_ref, iid_ref, tid_ref, img_ref, txt_ref, coef_ref)
    grad_ref[...] = lax.dot_general(
        coef_ref[...], img_ref[...], (((0,), (0,)), ((), ())), preferred_element_type=f32
    ).astype(bf16)


def last_kernel(
    scal_ref, iid_ref, tid_ref, img_ref, txt_ref, near_ref, cn_ref, gi_ref, grad_ref, coef_ref
):
    pair_kernel(scal_ref, iid_ref, tid_ref, img_ref, txt_ref, coef_ref, grad_ref)
    gi_ref[...] = (
        jnp.dot(cn_ref[...], near_ref[...], preferred_element_type=f32)
        + jnp.dot(coef_ref[...], txt_ref[...], preferred_element_type=f32)
    ).astype(bf16)


VMEM = pl.BlockSpec(memory_space=pltpu.VMEM)
SMEM = pl.BlockSpec(memory_space=pltpu.SMEM)


def pair_block(scal, image_ids, text_ids, images, texts, name):
    rows, width = images.shape
    cols = texts.shape[0]
    return pl.pallas_call(
        pair_kernel,
        in_specs=[SMEM] + [VMEM] * 4,
        out_specs=[VMEM] * 2,
        out_shape=[jax.ShapeDtypeStruct((rows, cols), bf16), jax.ShapeDtypeStruct((cols, width), bf16)],
        compiler_params=pltpu.CompilerParams(vmem_limit_bytes=LIMIT),
        cost_estimate=pl.CostEstimate(
            flops=4 * rows * cols * width, bytes_accessed=6 * rows * width, transcendentals=2 * rows * cols
        ),
        name=name,
    )(scal, image_ids, text_ids, images, texts)


def last_block(scal, image_ids, text_ids, images, texts, near, coef_near):
    rows, width = images.shape
    cols = texts.shape[0]
    return pl.pallas_call(
        last_kernel,
        in_specs=[SMEM] + [VMEM] * 6,
        out_specs=[VMEM] * 2,
        out_shape=[jax.ShapeDtypeStruct((rows, width), bf16), jax.ShapeDtypeStruct((cols, width), bf16)],
        scratch_shapes=[pltpu.VMEM((rows, cols), bf16)],
        compiler_params=pltpu.CompilerParams(vmem_limit_bytes=44 * 1024 * 1024),
        cost_estimate=pl.CostEstimate(
            flops=8 * rows * cols * width, bytes_accessed=10 * rows * width, transcendentals=2 * rows * cols
        ),
        name="far_pairs",
    )(scal, image_ids, text_ids, images, texts, near, coef_near)


def weight_kernel(own_ref, other_ref, low_ref, back_ref, bias_ref, out_ref):
    width, rows = own_ref.shape
    out_ref[:width, :] = (
        jnp.dot(own_ref[...], low_ref[...], preferred_element_type=f32)
        + jnp.dot(other_ref[...], back_ref[:rows, :], preferred_element_type=f32)
    ).astype(bf16)
    depth = out_ref.shape[0] - width
    row = lax.broadcasted_iota(jnp.int32, (depth, out_ref.shape[1]), 0)
    out_ref[width:, :] = jnp.where(row == 0, bias_ref[...], 0.0).astype(bf16)


def weight_grads(own_feats, other_feats, low, back, bias, tail):
    width, rows = own_feats.shape
    emb = low.shape[1]
    return pl.pallas_call(
        weight_kernel,
        in_specs=[VMEM] * 5,
        out_specs=VMEM,
        out_shape=jax.ShapeDtypeStruct((width + tail, emb), bf16),
        compiler_params=pltpu.CompilerParams(vmem_limit_bytes=LIMIT),
        cost_estimate=pl.CostEstimate(
            flops=4 * rows * width * emb, bytes_accessed=4 * width * emb, transcendentals=0
        ),
        name="weight_grads",
    )(own_feats, other_feats, low, back, bias)


def pick(parts, index):
    return lax.dynamic_index_in_dim(parts, index, 0, keepdims=False)


def normalized(raw):
    norm = jnp.sqrt(jnp.sum(raw * raw, axis=-1, keepdims=True) + 1e-06)
    return raw / norm, norm


def raw_gradient(unit_grad, unit, norm):
    return (unit_grad - unit * jnp.sum(unit * unit_grad, axis=-1, keepdims=True)) / norm


def local(
    image_feats,
    text_feats,
    image_proj,
    text_proj,
    image_bias,
    text_bias,
    image_ids,
    text_ids,
    log_scale,
    logit_bias,
):
    rows, width = image_feats.shape
    emb = image_proj.shape[1]
    half = rows // 2
    yh, x, c, yl = (lax.axis_index(a) for a in ("yh", "x", "c", "yl"))
    z = lax.axis_index(Z)
    n_yh, n_x, n_z = 2, 4, 8
    n_plane = n_yh * n_x * 2
    n_block = n_yh * n_x * 2

    grid = (n_yh, n_x, n_z, 2, 2, half)
    iids = image_ids.reshape(grid)
    iids = lax.dynamic_index_in_dim(iids, z, 2, keepdims=False)
    iids = lax.dynamic_index_in_dim(iids, c, 2, keepdims=False).reshape(1, -1)
    tids = text_ids.reshape(grid)
    tids = lax.dynamic_index_in_dim(tids, yh, 0, keepdims=False)
    tids = lax.dynamic_index_in_dim(tids, x, 0, keepdims=False)
    tids = lax.dynamic_index_in_dim(tids, yl, 2, keepdims=False)
    tids = jnp.concatenate([tids, tids], axis=0)
    tids = lax.dynamic_slice_in_dim(tids, z, n_z, 0)
    tids = jnp.stack([tids[p] for p in PLACES])
    near_ids = lax.dynamic_index_in_dim(tids, c, 1, keepdims=False).reshape(1, -1)
    far_ids = lax.dynamic_index_in_dim(tids, 1 - c, 1, keepdims=False).reshape(1, -1)
    scale = jnp.exp(log_scale[0])
    scal = jnp.stack([scale * LOG2E, logit_bias[0] * LOG2E, scale])

    image_part = jnp.dot(image_feats, image_proj, preferred_element_type=f32).reshape(2, half, emb)
    text_part = jnp.dot(text_feats, text_proj, preferred_element_type=f32).reshape(2, half, emb)
    image_got = exchange(pick(image_part, 1 - yl).astype(bf16), "yl")
    image_got, iids, near_ids, far_ids, scal = lax.optimization_barrier(
        (image_got, iids, near_ids, far_ids, scal)
    )
    image_raw = pick(image_part, yl) + image_got.astype(f32) + image_bias
    image_unit, image_norm = normalized(image_raw)
    image_copies = jnp.broadcast_to(image_unit.astype(bf16)[None], (n_plane, half, emb))
    image_copies, text_send, image_late, text_late = lax.optimization_barrier(
        (image_copies, pick(text_part, 1 - yl).astype(bf16), image_feats.T, text_feats.T)
    )
    text_got = exchange(text_send, "yl")
    text_raw = pick(text_part, yl) + text_got.astype(f32) + text_bias
    text_unit, text_norm = normalized(text_raw)

    images = lax.all_to_all(image_copies, PLANE, 0, 0).reshape(n_plane * half, emb)
    near = gather_ring(text_unit.astype(bf16), half)
    own_feats = jnp.where(c == 0, image_late, text_late)
    other_feats = exchange(jnp.where(c == 0, text_late, image_late), "c")
    images, near, own_feats, other_feats = lax.optimization_barrier((images, near, own_feats, other_feats))
    far = exchange(near, "c")
    coef_near, grad_near = pair_block(scal, iids, near_ids, images, near, "near_pairs")
    far, coef_near, grad_near = lax.optimization_barrier((far, coef_near, grad_near))
    grad_images, grad_far = last_block(scal, iids, far_ids, images, far, near, coef_near)

    grad_far = exchange(grad_far, "c")
    image_pieces = lax.all_to_all(grad_images.reshape(n_plane, half, emb), PLANE, 0, 0)
    text_held = (grad_near.astype(f32) + grad_far.astype(f32)).astype(bf16)
    text_sum = sum_ring(text_held, half)
    image_sum = jnp.sum(image_pieces.astype(f32), axis=0)
    image_grad = raw_gradient(image_sum, image_unit, image_norm)
    text_grad = raw_gradient(text_sum, text_unit, text_norm)
    pack = jnp.concatenate(
        [
            image_grad,
            text_grad,
            jnp.sum(image_grad, axis=0, keepdims=True),
            jnp.sum(text_grad, axis=0, keepdims=True),
            jnp.zeros((14, emb), f32),
        ],
        axis=0,
    ).astype(bf16)
    tail_rows = pack[2 * half :]
    send = jnp.concatenate([jnp.where(c == 0, pack[half : 2 * half], pack[:half]), tail_rows], axis=0)
    got = exchange(pack, "yl")
    back = exchange(send, "c")
    cross = lax.ppermute(send, ("c", "yl"), [(0, 3), (1, 2), (2, 1), (3, 0)])
    image_low = ordered(pack[:half], got[:half], yl)
    text_low = ordered(pack[half : 2 * half], got[half : 2 * half], yl)
    bias_own = tail_rows[:2].astype(f32) + got[2 * half : 2 * half + 2].astype(f32)
    bias_chip = bias_own + (back[half : half + 2].astype(f32) + cross[half : half + 2].astype(f32))

    grad_image_feats = lax.dot_general(
        image_low, image_proj, (((1,), (1,)), ((), ())), preferred_element_type=f32
    ).astype(bf16)
    grad_text_feats = lax.dot_general(
        text_low, text_proj, (((1,), (1,)), ((), ())), preferred_element_type=f32
    ).astype(bf16)

    own_low = jnp.where(c == 0, image_low, text_low)
    own_bias = lax.dynamic_slice_in_dim(bias_chip, c, 1, 0)
    tail = 4 * n_block
    payload = weight_grads(own_feats, other_feats, own_low, ordered(back[:half], cross[:half], yl), own_bias, tail)
    deep = (width + tail) // n_block
    pieces = lax.all_to_all(payload.reshape(n_block, deep, emb), BLOCK, 0, 0)
    pieces, grad_image_feats, grad_text_feats = lax.optimization_barrier(
        (pieces, grad_image_feats, grad_text_feats)
    )
    part = jnp.sum(pieces.astype(f32), axis=0).astype(bf16)
    one, two, three = (shift(part, "zz", d, 4).astype(f32) for d in (1, 2, 3))
    total = ((part.astype(f32) + two) + (one + three)).astype(bf16)
    total = spread(total, BLOCK, n_block).reshape(width + tail, emb)
    other = exchange(total, "c")
    return (
        grad_image_feats,
        grad_text_feats,
        jnp.where(c == 0, total[:width], other[:width]).astype(f32),
        jnp.where(c == 0, other[:width], total[:width]).astype(f32),
        jnp.where(c == 0, total[width], other[width]).astype(f32),
        jnp.where(c == 0, other[width], total[width]).astype(f32),
    )


def solution(mesh):
    fine = Mesh(mesh.devices.reshape(2, 4, 4, 2, 2, 2), ("yh", "x", "zz", "z0", "c", "yl"))
    batch = ("yh", "x", "zz", "z0", "c")
    in_specs = (
        P(batch, "yl"),
        P(batch, "yl"),
        P("yl", None),
        P("yl", None),
        P(),
        P(),
        P(),
        P(),
        P(),
        P(),
    )
    out_specs = (P(batch, "yl"), P(batch, "yl"), P("yl", None), P("yl", None), P(), P())
    return jax.shard_map(local, mesh=fine, in_specs=in_specs, out_specs=out_specs, check_vma=False)
```

```python
import functools

import jax
import jax.numpy as jnp
from jax import lax
from jax.experimental import pallas as pl
from jax.experimental.pallas import tpu as pltpu
from jax.sharding import Mesh
from jax.sharding import PartitionSpec as P

PLANE = ("yh", "x", "yl")
Z = ("zz", "z0")
BLOCK = ("yh", "x", "z0")
LIMIT = 24 * 1024 * 1024
LOG2E = 1.4426950408889634
bf16 = jnp.bfloat16
f32 = jnp.float32


def exchange(value, axis):
    return lax.ppermute(value, axis, [(0, 1), (1, 0)])


def shift(value, axes, step, count):
    return lax.ppermute(value, axes, [(i, (i + step) % count) for i in range(count)])


PLACES = (0, 4, 6, 2, 7, 3, 1, 5)


def gather_ring(own, half):
    across = shift(own, Z, 4, 8)
    behind = shift(own, Z, 2, 8)
    ahead = shift(own, Z, 6, 8)
    two = jnp.concatenate([own, across], axis=0)
    return jnp.concatenate([two, behind, ahead, shift(two, Z, 1, 8), shift(two, Z, 7, 8)], axis=0)


def sum_ring(held, half):
    ahead = shift(held[6 * half :], Z, 1, 8).astype(f32)
    behind = shift(held[4 * half : 6 * half], Z, 7, 8).astype(f32)
    far = shift(held[2 * half : 3 * half], Z, 6, 8).astype(f32)
    near = shift(held[3 * half : 4 * half], Z, 2, 8).astype(f32)
    across = held[half : 2 * half].astype(f32) + ahead[half:] + behind[half:]
    across = shift(across.astype(bf16), Z, 4, 8).astype(f32)
    return held[:half].astype(f32) + ahead[:half] + behind[:half] + far + near + across


def spread(block, axes, count):
    return lax.all_to_all(jnp.broadcast_to(block[None], (count,) + block.shape), axes, 0, 0)


def ordered(own, other, index):
    first = jnp.where(index == 0, own, other)
    second = jnp.where(index == 0, other, own)
    return jnp.concatenate([first, second], axis=0)


def coefs_of(scal_ref, iid_ref, tid_ref, img_ref, txt_ref, out_ref):
    rows = img_ref.shape[0]
    block = min(512, rows)
    s2 = scal_ref[0]
    b2 = scal_ref[1]
    s = scal_ref[2]
    for i in range(rows // block):
        part = pl.ds(i * block, block)
        iid = jnp.broadcast_to(iid_ref[:, i * block : (i + 1) * block], (8, block)).T[:, :1]
        dots = lax.dot_general(
            img_ref[part, :], txt_ref[...], (((1,), (1,)), ((), ())), preferred_element_type=f32
        )
        turn = jnp.where(iid == tid_ref[...], 1.0, -1.0)
        coef = (-s) * turn / (1.0 + jnp.exp2(turn * (dots * s2 + b2)))
        out_ref[part, :] = coef.astype(bf16)


def pair_kernel(scal_ref, iid_ref, tid_ref, img_ref, txt_ref, coef_ref, grad_ref):
    coefs_of(scal_ref, iid_ref, tid_ref, img_ref, txt_ref, coef_ref)
    grad_ref[...] = lax.dot_general(
        coef_ref[...], img_ref[...], (((0,), (0,)), ((), ())), preferred_element_type=f32
    ).astype(bf16)


def last_kernel(
    scal_ref, iid_ref, tid_ref, img_ref, txt_ref, near_ref, cn_ref, gi_ref, grad_ref, coef_ref
):
    pair_kernel(scal_ref, iid_ref, tid_ref, img_ref, txt_ref, coef_ref, grad_ref)
    gi_ref[...] = (
        jnp.dot(cn_ref[...], near_ref[...], preferred_element_type=f32)
        + jnp.dot(coef_ref[...], txt_ref[...], preferred_element_type=f32)
    ).astype(bf16)


VMEM = pl.BlockSpec(memory_space=pltpu.VMEM)
SMEM = pl.BlockSpec(memory_space=pltpu.SMEM)


def pair_block(scal, image_ids, text_ids, images, texts, name):
    rows, width = images.shape
    cols = texts.shape[0]
    return pl.pallas_call(
        pair_kernel,
        in_specs=[SMEM] + [VMEM] * 4,
        out_specs=[VMEM] * 2,
        out_shape=[jax.ShapeDtypeStruct((rows, cols), bf16), jax.ShapeDtypeStruct((cols, width), bf16)],
        compiler_params=pltpu.CompilerParams(vmem_limit_bytes=LIMIT),
        cost_estimate=pl.CostEstimate(
            flops=4 * rows * cols * width, bytes_accessed=6 * rows * width, transcendentals=2 * rows * cols
        ),
        name=name,
    )(scal, image_ids, text_ids, images, texts)


def last_block(scal, image_ids, text_ids, images, texts, near, coef_near):
    rows, width = images.shape
    cols = texts.shape[0]
    return pl.pallas_call(
        last_kernel,
        in_specs=[SMEM] + [VMEM] * 6,
        out_specs=[VMEM] * 2,
        out_shape=[jax.ShapeDtypeStruct((rows, width), bf16), jax.ShapeDtypeStruct((cols, width), bf16)],
        scratch_shapes=[pltpu.VMEM((rows, cols), bf16)],
        compiler_params=pltpu.CompilerParams(vmem_limit_bytes=44 * 1024 * 1024),
        cost_estimate=pl.CostEstimate(
            flops=8 * rows * cols * width, bytes_accessed=10 * rows * width, transcendentals=2 * rows * cols
        ),
        name="far_pairs",
    )(scal, image_ids, text_ids, images, texts, near, coef_near)


def weight_kernel(own_ref, other_ref, low_ref, back_ref, bias_ref, out_ref):
    width, rows = own_ref.shape
    out_ref[:width, :] = (
        jnp.dot(own_ref[...], low_ref[...], preferred_element_type=f32)
        + jnp.dot(other_ref[...], back_ref[:rows, :], preferred_element_type=f32)
    ).astype(bf16)
    depth = out_ref.shape[0] - width
    row = lax.broadcasted_iota(jnp.int32, (depth, out_ref.shape[1]), 0)
    out_ref[width:, :] = jnp.where(row == 0, bias_ref[...], 0.0).astype(bf16)


def weight_grads(own_feats, other_feats, low, back, bias, tail):
    width, rows = own_feats.shape
    emb = low.shape[1]
    return pl.pallas_call(
        weight_kernel,
        in_specs=[VMEM] * 5,
        out_specs=VMEM,
        out_shape=jax.ShapeDtypeStruct((width + tail, emb), bf16),
        compiler_params=pltpu.CompilerParams(vmem_limit_bytes=LIMIT),
        cost_estimate=pl.CostEstimate(
            flops=4 * rows * width * emb, bytes_accessed=4 * width * emb, transcendentals=0
        ),
        name="weight_grads",
    )(own_feats, other_feats, low, back, bias)


def pick(parts, index):
    return lax.dynamic_index_in_dim(parts, index, 0, keepdims=False)


def normalized(raw):
    norm = jnp.sqrt(jnp.sum(raw * raw, axis=-1, keepdims=True) + 1e-06)
    return raw / norm, norm


def raw_gradient(unit_grad, unit, norm):
    return (unit_grad - unit * jnp.sum(unit * unit_grad, axis=-1, keepdims=True)) / norm


def local(
    image_feats,
    text_feats,
    image_proj,
    text_proj,
    image_bias,
    text_bias,
    image_ids,
    text_ids,
    log_scale,
    logit_bias,
):
    rows, width = image_feats.shape
    emb = image_proj.shape[1]
    half = rows // 2
    yh, x, c, yl = (lax.axis_index(a) for a in ("yh", "x", "c", "yl"))
    z = lax.axis_index(Z)
    n_yh, n_x, n_z = 2, 4, 8
    n_plane = n_yh * n_x * 2
    n_block = n_yh * n_x * 2

    grid = (n_yh, n_x, n_z, 2, 2, half)
    iids = image_ids.reshape(grid)
    iids = lax.dynamic_index_in_dim(iids, z, 2, keepdims=False)
    iids = lax.dynamic_index_in_dim(iids, c, 2, keepdims=False).reshape(1, -1)
    tids = text_ids.reshape(grid)
    tids = lax.dynamic_index_in_dim(tids, yh, 0, keepdims=False)
    tids = lax.dynamic_index_in_dim(tids, x, 0, keepdims=False)
    tids = lax.dynamic_index_in_dim(tids, yl, 2, keepdims=False)
    tids = jnp.concatenate([tids, tids], axis=0)
    tids = lax.dynamic_slice_in_dim(tids, z, n_z, 0)
    tids = jnp.stack([tids[p] for p in PLACES])
    near_ids = lax.dynamic_index_in_dim(tids, c, 1, keepdims=False).reshape(1, -1)
    far_ids = lax.dynamic_index_in_dim(tids, 1 - c, 1, keepdims=False).reshape(1, -1)
    scale = jnp.exp(log_scale[0])
    scal = jnp.stack([scale * LOG2E, logit_bias[0] * LOG2E, scale])

    image_part = jnp.dot(image_feats, image_proj, preferred_element_type=f32).reshape(2, half, emb)
    text_part = jnp.dot(text_feats, text_proj, preferred_element_type=f32).reshape(2, half, emb)
    image_got = exchange(pick(image_part, 1 - yl).astype(bf16), "yl")
    image_got, iids, near_ids, far_ids, scal = lax.optimization_barrier(
        (image_got, iids, near_ids, far_ids, scal)
    )
    image_raw = pick(image_part, yl) + image_got.astype(f32) + image_bias
    image_unit, image_norm = normalized(image_raw)
    image_copies = jnp.broadcast_to(image_unit.astype(bf16)[None], (n_plane, half, emb))
    image_copies, text_send, image_late, text_late = lax.optimization_barrier(
        (image_copies, pick(text_part, 1 - yl).astype(bf16), image_feats.T, text_feats.T)
    )
    text_got = exchange(text_send, "yl")
    text_raw = pick(text_part, yl) + text_got.astype(f32) + text_bias
    text_unit, text_norm = normalized(text_raw)

    images = lax.all_to_all(image_copies, PLANE, 0, 0).reshape(n_plane * half, emb)
    near = gather_ring(text_unit.astype(bf16), half)
    own_feats = jnp.where(c == 0, image_late, text_late)
    other_feats = exchange(jnp.where(c == 0, text_late, image_late), "c")
    images, near, own_feats, other_feats = lax.optimization_barrier((images, near, own_feats, other_feats))
    far = exchange(near, "c")
    coef_near, grad_near = pair_block(scal, iids, near_ids, images, near, "near_pairs")
    far, coef_near, grad_near = lax.optimization_barrier((far, coef_near, grad_near))
    grad_images, grad_far = last_block(scal, iids, far_ids, images, far, near, coef_near)

    grad_far = exchange(grad_far, "c")
    image_pieces = lax.all_to_all(grad_images.reshape(n_plane, half, emb), PLANE, 0, 0)
    text_held = (grad_near.astype(f32) + grad_far.astype(f32)).astype(bf16)
    text_sum = sum_ring(text_held, half)
    image_sum = jnp.sum(image_pieces.astype(f32), axis=0)
    image_grad = raw_gradient(image_sum, image_unit, image_norm)
    text_grad = raw_gradient(text_sum, text_unit, text_norm)
    pack = jnp.concatenate(
        [
            image_grad,
            text_grad,
            jnp.sum(image_grad, axis=0, keepdims=True),
            jnp.sum(text_grad, axis=0, keepdims=True),
            jnp.zeros((14, emb), f32),
        ],
        axis=0,
    ).astype(bf16)
    got = exchange(pack, "yl")
    image_low = ordered(pack[:half], got[:half], yl)
    text_low = ordered(pack[half : 2 * half], got[half : 2 * half], yl)
    bias_rows = pack[2 * half : 2 * half + 2].astype(f32) + got[2 * half : 2 * half + 2].astype(f32)

    grad_image_feats = lax.dot_general(
        image_low, image_proj, (((1,), (1,)), ((), ())), preferred_element_type=f32
    ).astype(bf16)
    grad_text_feats = lax.dot_general(
        text_low, text_proj, (((1,), (1,)), ((), ())), preferred_element_type=f32
    ).astype(bf16)

    extra = jnp.concatenate([bias_rows, jnp.zeros((14, emb), f32)], axis=0).astype(bf16)
    send = jnp.concatenate([jnp.where(c == 0, text_low, image_low), extra], axis=0)
    back = exchange(send, "c")
    own_low = jnp.where(c == 0, image_low, text_low)
    bias_chip = bias_rows + back[rows : rows + 2].astype(f32)
    own_bias = lax.dynamic_slice_in_dim(bias_chip, c, 1, 0)
    tail = 4 * n_block
    payload = weight_grads(own_feats, other_feats, own_low, back, own_bias, tail)
    deep = (width + tail) // n_block
    pieces = lax.all_to_all(payload.reshape(n_block, deep, emb), BLOCK, 0, 0)
    pieces, grad_image_feats, grad_text_feats = lax.optimization_barrier(
        (pieces, grad_image_feats, grad_text_feats)
    )
    part = jnp.sum(pieces.astype(f32), axis=0).astype(bf16)
    one, two, three = (shift(part, "zz", d, 4).astype(f32) for d in (1, 2, 3))
    total = ((part.astype(f32) + two) + (one + three)).astype(bf16)
    total = spread(total, BLOCK, n_block).reshape(width + tail, emb)
    other = exchange(total, "c")
    return (
        grad_image_feats,
        grad_text_feats,
        jnp.where(c == 0, total[:width], other[:width]).astype(f32),
        jnp.where(c == 0, other[:width], total[:width]).astype(f32),
        jnp.where(c == 0, total[width], other[width]).astype(f32),
        jnp.where(c == 0, other[width], total[width]).astype(f32),
    )


def solution(mesh):
    fine = Mesh(mesh.devices.reshape(2, 4, 4, 2, 2, 2), ("yh", "x", "zz", "z0", "c", "yl"))
    batch = ("yh", "x", "zz", "z0", "c")
    in_specs = (
        P(batch, "yl"),
        P(batch, "yl"),
        P("yl", None),
        P("yl", None),
        P(),
        P(),
        P(),
        P(),
        P(),
        P(),
    )
    out_specs = (P(batch, "yl"), P(batch, "yl"), P("yl", None), P("yl", None), P(), P())
    return jax.shard_map(local, mesh=fine, in_specs=in_specs, out_specs=out_specs, check_vma=False)
```

```python
import functools

import jax
import jax.numpy as jnp
from jax import lax
from jax.experimental import pallas as pl
from jax.experimental.pallas import tpu as pltpu
from jax.sharding import Mesh
from jax.sharding import PartitionSpec as P

PLANE = ("yh", "x", "yl")
Z = ("zz", "z0")
BLOCK = ("yh", "x", "z0")
LIMIT = 24 * 1024 * 1024
LOG2E = 1.4426950408889634
bf16 = jnp.bfloat16
f32 = jnp.float32


def exchange(value, axis):
    return lax.ppermute(value, axis, [(0, 1), (1, 0)])


def shift(value, axes, step, count):
    return lax.ppermute(value, axes, [(i, (i + step) % count) for i in range(count)])


PLACES = (0, 4, 6, 2, 7, 3, 1, 5)


def gather_ring(own, half):
    across = shift(own, Z, 4, 8)
    behind = shift(own, Z, 2, 8)
    ahead = shift(own, Z, 6, 8)
    two = jnp.concatenate([own, across], axis=0)
    return jnp.concatenate([two, behind, ahead, shift(two, Z, 1, 8), shift(two, Z, 7, 8)], axis=0)


def sum_ring(held, half):
    ahead = shift(held[6 * half :], Z, 1, 8).astype(f32)
    behind = shift(held[4 * half : 6 * half], Z, 7, 8).astype(f32)
    far = shift(held[2 * half : 3 * half], Z, 6, 8).astype(f32)
    near = shift(held[3 * half : 4 * half], Z, 2, 8).astype(f32)
    across = held[half : 2 * half].astype(f32) + ahead[half:] + behind[half:]
    across = shift(across.astype(bf16), Z, 4, 8).astype(f32)
    return held[:half].astype(f32) + ahead[:half] + behind[:half] + far + near + across


def spread(block, axes, count):
    return lax.all_to_all(jnp.broadcast_to(block[None], (count,) + block.shape), axes, 0, 0)


def ordered(own, other, index):
    first = jnp.where(index == 0, own, other)
    second = jnp.where(index == 0, other, own)
    return jnp.concatenate([first, second], axis=0)


def coefs_of(scal_ref, iid_ref, tid_ref, img_ref, txt_ref, out_ref):
    rows = img_ref.shape[0]
    block = min(512, rows)
    s2 = scal_ref[0]
    b2 = scal_ref[1]
    s = scal_ref[2]
    for i in range(rows // block):
        part = pl.ds(i * block, block)
        iid = jnp.broadcast_to(iid_ref[:, i * block : (i + 1) * block], (8, block)).T[:, :1]
        dots = lax.dot_general(
            img_ref[part, :], txt_ref[...], (((1,), (1,)), ((), ())), preferred_element_type=f32
        )
        turn = jnp.where(iid == tid_ref[...], 1.0, -1.0)
        coef = (-s) * turn / (1.0 + jnp.exp2(turn * (dots * s2 + b2)))
        out_ref[part, :] = coef.astype(bf16)


def pair_kernel(scal_ref, iid_ref, tid_ref, img_ref, txt_ref, coef_ref, grad_ref):
    coefs_of(scal_ref, iid_ref, tid_ref, img_ref, txt_ref, coef_ref)
    grad_ref[...] = lax.dot_general(
        coef_ref[...], img_ref[...], (((0,), (0,)), ((), ())), preferred_element_type=f32
    ).astype(bf16)


def last_kernel(
    scal_ref, iid_ref, tid_ref, img_ref, txt_ref, near_ref, cn_ref, room_ref, gi_ref, grad_ref, coef_ref
):
    pair_kernel(scal_ref, iid_ref, tid_ref, img_ref, txt_ref, coef_ref, grad_ref)
    gi_ref[...] = (
        jnp.dot(cn_ref[...], near_ref[...], preferred_element_type=f32)
        + jnp.dot(coef_ref[...], txt_ref[...], preferred_element_type=f32)
    ).astype(bf16)


VMEM = pl.BlockSpec(memory_space=pltpu.VMEM)
SMEM = pl.BlockSpec(memory_space=pltpu.SMEM)


def pair_block(scal, image_ids, text_ids, images, texts, name):
    rows, width = images.shape
    cols = texts.shape[0]
    return pl.pallas_call(
        pair_kernel,
        in_specs=[SMEM] + [VMEM] * 4,
        out_specs=[VMEM] * 2,
        out_shape=[jax.ShapeDtypeStruct((rows, cols), bf16), jax.ShapeDtypeStruct((cols, width), bf16)],
        compiler_params=pltpu.CompilerParams(vmem_limit_bytes=LIMIT),
        cost_estimate=pl.CostEstimate(
            flops=4 * rows * cols * width, bytes_accessed=6 * rows * width, transcendentals=2 * rows * cols
        ),
        name=name,
    )(scal, image_ids, text_ids, images, texts)


def last_block(scal, image_ids, text_ids, images, texts, near, coef_near, room):
    rows, width = images.shape
    cols = texts.shape[0]
    return pl.pallas_call(
        last_kernel,
        in_specs=[SMEM] + [VMEM] * 6 + [pl.BlockSpec(memory_space=pl.ANY)],
        out_specs=[VMEM] * 2,
        out_shape=[jax.ShapeDtypeStruct((rows, width), bf16), jax.ShapeDtypeStruct((cols, width), bf16)],
        scratch_shapes=[pltpu.VMEM((rows, cols), bf16)],
        compiler_params=pltpu.CompilerParams(vmem_limit_bytes=44 * 1024 * 1024),
        cost_estimate=pl.CostEstimate(
            flops=8 * rows * cols * width, bytes_accessed=10 * rows * width, transcendentals=2 * rows * cols
        ),
        input_output_aliases={7: 0},
        name="far_pairs",
    )(scal, image_ids, text_ids, images, texts, near, coef_near, room)


def weight_kernel(own_ref, other_ref, low_ref, back_ref, bias_ref, out_ref):
    width, rows = own_ref.shape
    out_ref[:width, :] = (
        jnp.dot(own_ref[...], low_ref[...], preferred_element_type=f32)
        + jnp.dot(other_ref[...], back_ref[:rows, :], preferred_element_type=f32)
    ).astype(bf16)
    depth = out_ref.shape[0] - width
    row = lax.broadcasted_iota(jnp.int32, (depth, out_ref.shape[1]), 0)
    out_ref[width:, :] = jnp.where(row == 0, bias_ref[...], 0.0).astype(bf16)


def weight_grads(own_feats, other_feats, low, back, bias, tail):
    width, rows = own_feats.shape
    emb = low.shape[1]
    return pl.pallas_call(
        weight_kernel,
        in_specs=[VMEM] * 5,
        out_specs=VMEM,
        out_shape=jax.ShapeDtypeStruct((width + tail, emb), bf16),
        compiler_params=pltpu.CompilerParams(vmem_limit_bytes=LIMIT),
        cost_estimate=pl.CostEstimate(
            flops=4 * rows * width * emb, bytes_accessed=4 * width * emb, transcendentals=0
        ),
        name="weight_grads",
    )(own_feats, other_feats, low, back, bias)


def pick(parts, index):
    return lax.dynamic_index_in_dim(parts, index, 0, keepdims=False)


def normalized(raw):
    norm = jnp.sqrt(jnp.sum(raw * raw, axis=-1, keepdims=True) + 1e-06)
    return raw / norm, norm


def raw_gradient(unit_grad, unit, norm):
    return (unit_grad - unit * jnp.sum(unit * unit_grad, axis=-1, keepdims=True)) / norm


def local(
    image_feats,
    text_feats,
    image_proj,
    text_proj,
    image_bias,
    text_bias,
    image_ids,
    text_ids,
    log_scale,
    logit_bias,
):
    rows, width = image_feats.shape
    emb = image_proj.shape[1]
    half = rows // 2
    yh, x, c, yl = (lax.axis_index(a) for a in ("yh", "x", "c", "yl"))
    z = lax.axis_index(Z)
    n_yh, n_x, n_z = 2, 4, 8
    n_plane = n_yh * n_x * 2
    n_block = n_yh * n_x * 2

    grid = (n_yh, n_x, n_z, 2, 2, half)
    iids = image_ids.reshape(grid)
    iids = lax.dynamic_index_in_dim(iids, z, 2, keepdims=False)
    iids = lax.dynamic_index_in_dim(iids, c, 2, keepdims=False).reshape(1, -1)
    tids = text_ids.reshape(grid)
    tids = lax.dynamic_index_in_dim(tids, yh, 0, keepdims=False)
    tids = lax.dynamic_index_in_dim(tids, x, 0, keepdims=False)
    tids = lax.dynamic_index_in_dim(tids, yl, 2, keepdims=False)
    tids = jnp.concatenate([tids, tids], axis=0)
    tids = lax.dynamic_slice_in_dim(tids, z, n_z, 0)
    tids = jnp.stack([tids[p] for p in PLACES])
    near_ids = lax.dynamic_index_in_dim(tids, c, 1, keepdims=False).reshape(1, -1)
    far_ids = lax.dynamic_index_in_dim(tids, 1 - c, 1, keepdims=False).reshape(1, -1)
    scale = jnp.exp(log_scale[0])
    scal = jnp.stack([scale * LOG2E, logit_bias[0] * LOG2E, scale])

    image_part = jnp.dot(image_feats, image_proj, preferred_element_type=f32).reshape(2, half, emb)
    text_part = jnp.dot(text_feats, text_proj, preferred_element_type=f32).reshape(2, half, emb)
    image_got = exchange(pick(image_part, 1 - yl).astype(bf16), "yl")
    image_got, iids, near_ids, far_ids, scal = lax.optimization_barrier(
        (image_got, iids, near_ids, far_ids, scal)
    )
    image_raw = pick(image_part, yl) + image_got.astype(f32) + image_bias
    image_unit, image_norm = normalized(image_raw)
    image_copies = jnp.broadcast_to(image_unit.astype(bf16)[None], (n_plane, half, emb))
    image_copies, text_send, image_late, text_late = lax.optimization_barrier(
        (image_copies, pick(text_part, 1 - yl).astype(bf16), image_feats.T, text_feats.T)
    )
    text_got = exchange(text_send, "yl")
    text_raw = pick(text_part, yl) + text_got.astype(f32) + text_bias
    text_unit, text_norm = normalized(text_raw)

    images = lax.all_to_all(image_copies, PLANE, 0, 0).reshape(n_plane * half, emb)
    near = gather_ring(text_unit.astype(bf16), half)
    own_feats = jnp.where(c == 0, image_late, text_late)
    other_feats = exchange(jnp.where(c == 0, text_late, image_late), "c")
    images, near, own_feats, other_feats = lax.optimization_barrier((images, near, own_feats, other_feats))
    far = exchange(near, "c")
    coef_near, grad_near = pair_block(scal, iids, near_ids, images, near, "near_pairs")
    far, coef_near, grad_near = lax.optimization_barrier((far, coef_near, grad_near))
    grad_images, grad_far = last_block(
        scal, iids, far_ids, images, far, near, coef_near, image_copies.reshape(n_plane * half, emb)
    )

    grad_far = exchange(grad_far, "c")
    image_pieces = lax.all_to_all(grad_images.reshape(n_plane, half, emb), PLANE, 0, 0)
    text_held = (grad_near.astype(f32) + grad_far.astype(f32)).astype(bf16)
    text_sum = sum_ring(text_held, half)
    image_sum = jnp.sum(image_pieces.astype(f32), axis=0)
    image_grad = raw_gradient(image_sum, image_unit, image_norm)
    text_grad = raw_gradient(text_sum, text_unit, text_norm)
    pack = jnp.concatenate(
        [
            image_grad,
            text_grad,
            jnp.sum(image_grad, axis=0, keepdims=True),
            jnp.sum(text_grad, axis=0, keepdims=True),
            jnp.zeros((14, emb), f32),
        ],
        axis=0,
    ).astype(bf16)
    got = exchange(pack, "yl")
    image_low = ordered(pack[:half], got[:half], yl)
    text_low = ordered(pack[half : 2 * half], got[half : 2 * half], yl)
    bias_rows = pack[2 * half : 2 * half + 2].astype(f32) + got[2 * half : 2 * half + 2].astype(f32)

    grad_image_feats = lax.dot_general(
        image_low, image_proj, (((1,), (1,)), ((), ())), preferred_element_type=f32
    ).astype(bf16)
    grad_text_feats = lax.dot_general(
        text_low, text_proj, (((1,), (1,)), ((), ())), preferred_element_type=f32
    ).astype(bf16)

    extra = jnp.concatenate([bias_rows, jnp.zeros((14, emb), f32)], axis=0).astype(bf16)
    send = jnp.concatenate([jnp.where(c == 0, text_low, image_low), extra], axis=0)
    back = exchange(send, "c")
    own_low = jnp.where(c == 0, image_low, text_low)
    bias_chip = bias_rows + back[rows : rows + 2].astype(f32)
    own_bias = lax.dynamic_slice_in_dim(bias_chip, c, 1, 0)
    tail = 4 * n_block
    payload = weight_grads(own_feats, other_feats, own_low, back, own_bias, tail)
    deep = (width + tail) // n_block
    pieces = lax.all_to_all(payload.reshape(n_block, deep, emb), BLOCK, 0, 0)
    pieces, grad_image_feats, grad_text_feats = lax.optimization_barrier(
        (pieces, grad_image_feats, grad_text_feats)
    )
    part = jnp.sum(pieces.astype(f32), axis=0).astype(bf16)
    one, two, three = (shift(part, "zz", d, 4).astype(f32) for d in (1, 2, 3))
    total = ((part.astype(f32) + two) + (one + three)).astype(bf16)
    total = spread(total, BLOCK, n_block).reshape(width + tail, emb)
    other = exchange(total, "c")
    return (
        grad_image_feats,
        grad_text_feats,
        jnp.where(c == 0, total[:width], other[:width]).astype(f32),
        jnp.where(c == 0, other[:width], total[:width]).astype(f32),
        jnp.where(c == 0, total[width], other[width]).astype(f32),
        jnp.where(c == 0, other[width], total[width]).astype(f32),
    )


def solution(mesh):
    fine = Mesh(mesh.devices.reshape(2, 4, 4, 2, 2, 2), ("yh", "x", "zz", "z0", "c", "yl"))
    batch = ("yh", "x", "zz", "z0", "c")
    in_specs = (
        P(batch, "yl"),
        P(batch, "yl"),
        P("yl", None),
        P("yl", None),
        P(),
        P(),
        P(),
        P(),
        P(),
        P(),
    )
    out_specs = (P(batch, "yl"), P(batch, "yl"), P("yl", None), P("yl", None), P(), P())
    return jax.shard_map(local, mesh=fine, in_specs=in_specs, out_specs=out_specs, check_vma=False)
```
